512 devices in a mesh: coef: 8 (over y, x_lo), grid: 64 (over z, x_hi, core).
Axes of the slice: x: 4 (x_hi: 2, x_lo: 2; x = x_hi * 2 + x_lo), y: 4, z: 16, core: 2. Of those that a mesh axis runs over, the one named last changes fastest.
Arguments:
- basis_values: bfloat16 [40960, 2688], P('grid'), may hold values from -6 to 6
- occ_coef: bfloat16 [40960, 1024], P('grid', 'coef'), may hold values from -0.125 to 0.125
- listed_panels: int32 [64, 21], P('grid'), may hold values from 0 to 319, as said below
- centres: float32 [3, 40960], replicated, may hold values from 0 to 4
- point_weights: float32 [40960], P('grid'), may hold values from 0.25 to 4
Outputs:
- exchange_tiles: float32 [40960, 1024], P('grid', 'coef')
The draws below stay inside these ranges and needn't reach their ends.
Inputs may be any that keep to these rules, and one draw needn't show every extreme that they name: `listed_panels`: the panels of one batch are distinct; panel p belongs to batch p // 5, and batch b names only panels of batches b - 4 to b + 4.
All inputs are finite; a program needn't handle non-finite values.
Results may differ from the reference program's by a relative error of at most 0.0085.
Values may be sent and summed in bfloat16 or wider, within the bound.
A program may use at most 64 MiB of HBM per device.

```python
import math
import jax
import jax.numpy as jnp
from jax import lax

ORBITALS = 1024
PANEL_ROWS = 128
PANELS_DEV = 5
REACH = 4
LISTED = 21
POINTS_DEV = 640
PANELS = 320
FUNCTIONS = 40960
POINTS = 40960
N_COEF = 8
N_GRID = 64


def draw_listed_panels(key, part):
    batches = jnp.arange(N_GRID, dtype=jnp.int32)
    slots = jnp.arange((2 * REACH + 1) * PANELS_DEV, dtype=jnp.int32)
    candidates = (batches[:, None] - REACH) * PANELS_DEV + slots[None, :]
    valid = (candidates >= 0) & (candidates < PANELS)
    noise = jax.random.randint(key, candidates.shape, 0, 2 ** 20, dtype=jnp.int32)
    scores = jnp.where(valid, noise * 64 + slots[None, :], -1)
    picked = lax.top_k(scores, LISTED)[1]
    return jnp.take_along_axis(candidates, picked, axis=1).astype(jnp.int32)


def block_levels(own_key, dims, cuts, least, largest):
    factor_of, own = 1.0, jax.random.fold_in(own_key, 6)
    for dim, parts in cuts:
        steps = jnp.exp(jax.random.uniform(jax.random.fold_in(own, dim), (parts,), jnp.float32, least / len(cuts), largest / len(cuts)))
        factor_of = factor_of * jnp.repeat(steps, dims[dim] // parts).reshape([-1 if axis == dim else 1 for axis in range(len(dims))])
    return factor_of


def centred(own_key, dims, spread, most, split=(), kind=jnp.bfloat16):
    gain = block_levels(own_key, dims, split, -0.22, 0.18) if split else 1.0
    values = jax.random.normal(own_key, dims, jnp.float32) * spread * gain
    return jnp.minimum(jnp.maximum(values, -most), most).astype(kind)


def setup_inputs(seed: int = 0) -> dict:
    seeds = jax.random.split(jax.random.key(seed), 6)
    return {
        "basis_values": centred(seeds[0], (POINTS, LISTED * PANEL_ROWS), 1.0, 6.0, ((0, 64),)),
        "occ_coef": centred(seeds[1], (FUNCTIONS, ORBITALS), (LISTED * PANEL_ROWS) ** -0.5, 0.125, ((0, 64), (1, 8))),
        "listed_panels": draw_listed_panels(jax.random.fold_in(seeds[5], 71), 0),
        "centres": jnp.clip(jax.random.uniform(seeds[3], (3, POINTS), jnp.float32, 0.0, 4.0), 0.0, 4.0),
        "point_weights": jnp.clip(jnp.exp(math.log(4.0) - 2.7725887 * jax.random.uniform(seeds[4], (POINTS,), jnp.float32) ** block_levels(seeds[4], (POINTS,), ((0, 64),), -0.2, 0.2)), 0.25, 4.0),
    }


def reference(basis_values, occ_coef, listed_panels, centres, point_weights):
    panels = occ_coef.reshape(PANELS, PANEL_ROWS, ORBITALS)
    block = ORBITALS // N_COEF
    anchor = jnp.zeros((), jnp.int32)

    def orbital_field(batch):
        start = (batch * POINTS_DEV).astype(jnp.int32)
        rows = lax.dynamic_slice_in_dim(basis_values, start, POINTS_DEV, 0)
        chosen = jnp.take(panels, listed_panels[batch], axis=0).reshape(LISTED * PANEL_ROWS, ORBITALS)
        return jnp.dot(rows, chosen, preferred_element_type=jnp.float32).astype(jnp.bfloat16)
    fields = lax.map(orbital_field, jnp.arange(N_GRID, dtype=jnp.int32))
    zeros = jnp.zeros((1, POINTS_DEV, ORBITALS), jnp.bfloat16)
    padded = jnp.concatenate([zeros, fields, zeros], 0)
    padded_centres = jnp.pad(centres, ((0, 0), (POINTS_DEV, POINTS_DEV)))

    def step(total, batch):
        start = (batch * POINTS_DEV).astype(jnp.int32)
        own = padded[batch + 1]
        near = lax.dynamic_slice_in_dim(padded, batch.astype(jnp.int32), 3, 0).reshape(3 * POINTS_DEV, ORBITALS)
        density = jnp.zeros((POINTS_DEV, 3 * POINTS_DEV), jnp.float32)
        for part in range(N_COEF):
            left = own[:, part * block:(part + 1) * block]
            right = near[:, part * block:(part + 1) * block]
            term = lax.dot_general(left, right, (((1,), (1,)), ((), ())), preferred_element_type=jnp.float32)
            term = lax.optimization_barrier((term / jnp.sqrt(jnp.float32(ORBITALS))).astype(jnp.bfloat16))
            density = density + term.astype(jnp.float32)
        own_centres = lax.dynamic_slice(centres, (anchor, start), (3, POINTS_DEV))
        near_centres = lax.dynamic_slice(padded_centres, (anchor, start), (3, 3 * POINTS_DEV))
        distance = jnp.zeros((POINTS_DEV, 3 * POINTS_DEV), jnp.float32)
        for axis in range(3):
            gap = own_centres[axis][:, None] - near_centres[axis][None, :]
            distance = distance + gap * gap
        kernel = 1.0 / jnp.sqrt(distance + 0.25)
        mixed = (kernel * density).astype(jnp.bfloat16)
        exchanged = jnp.dot(mixed, near, preferred_element_type=jnp.float32)
        weights = lax.dynamic_slice_in_dim(point_weights, start, POINTS_DEV, 0)
        weighted = (exchanged * weights[:, None] / jnp.sqrt(jnp.float32(3 * POINTS_DEV))).astype(jnp.bfloat16)
        rows = lax.dynamic_slice_in_dim(basis_values, start, POINTS_DEV, 0)
        tiles = lax.dot_general(rows, weighted, (((0,), (0,)), ((), ())), preferred_element_type=jnp.float32)
        tiles = tiles / jnp.sqrt(jnp.float32(POINTS_DEV))
        total = total.at[listed_panels[batch]].add(tiles.reshape(LISTED, PANEL_ROWS, ORBITALS))
        return (total, None)
    begin = jnp.zeros((PANELS, PANEL_ROWS, ORBITALS), jnp.float32)
    total, unused = lax.scan(step, begin, jnp.arange(N_GRID, dtype=jnp.int32))
    return total.reshape(FUNCTIONS, ORBITALS)
```

```python
import functools
import math

import jax
import jax.numpy as jnp
from jax import lax
from jax.experimental import pallas as pl
from jax.experimental.pallas import tpu as pltpu
from jax.sharding import PartitionSpec as P

PANEL_ROWS = 128
PANELS_DEV = 5
LISTED = 21
PAIRS = (-2, -1, 1, 2)
ROW_PARTS = 2
MESH = pl.DeviceIdType.MESH


def fused(
    nc, ng, orbitals,
    basis_hbm, occ_hbm, listed, centres_hbm, weights_hbm, out_ref,
    basis, basis_t, cand, chosen, coords, columns, inverse, near_own, near_par,
    ext_rows, kern_own, kern_par, kern_ext, send_own, send_ext, got_own, got_ext,
    weighted, tiles, to_mate, from_mate, to_owner, from_owner,
    local_sem, occ_send, occ_recv, mate_send, mate_recv,
    field_send, field_recv, pass_send, pass_recv, ext_send, ext_recv,
    own_send, own_recv, back_send, back_recv,
    comb_send, comb_recv, final_send, final_recv,
):
    points, width = near_own.shape[1:]
    rows = points // nc
    part = points // ROW_PARTS
    c = lax.axis_index("coef")
    b = lax.axis_index("grid")
    k = lax.rem(b, 2)
    mate = b + 1 - 2 * k
    outer = lax.rem(b - 1 + 2 * k + ng, ng)

    def at(coef, grid):
        return {"coef": coef, "grid": grid}

    def pair(d):
        return lax.rem(b + 2 * d + ng, ng)

    def remote(src, dst, send, recv, to):
        return pltpu.make_async_remote_copy(
            src_ref=src, dst_ref=dst, send_sem=send, recv_sem=recv, device_id=to, device_id_type=MESH
        )

    def coef_of(j):
        return lax.rem(c + j, nc)

    loads = [
        pltpu.make_async_copy(basis_hbm, basis, local_sem.at[0]),
        pltpu.make_async_copy(occ_hbm, cand.at[pl.ds(PANELS_DEV * (4 + k), PANELS_DEV)], local_sem.at[1]),
        pltpu.make_async_copy(centres_hbm.at[:, pl.ds(pl.multiple_of(b * points, 128), points)], coords.at[0, pl.ds(0, 3)], local_sem.at[2]),
        pltpu.make_async_copy(centres_hbm.at[:, pl.ds(pl.multiple_of(mate * points, 128), points)], coords.at[1, pl.ds(0, 3)], local_sem.at[3]),
        pltpu.make_async_copy(centres_hbm.at[:, pl.ds(pl.multiple_of(outer * points, 128), points)], coords.at[2, pl.ds(0, 3)], local_sem.at[4]),
        pltpu.make_async_copy(weights_hbm, coords.at[0, pl.ds(3, 1)], local_sem.at[5]),
    ]
    coords[...] = jnp.zeros_like(coords)
    for load in loads:
        load.start()

    barrier = pltpu.get_barrier_semaphore()
    pl.semaphore_signal(barrier, inc=1, device_id=at(c, mate), device_id_type=MESH)
    for d in PAIRS:
        pl.semaphore_signal(barrier, inc=1, device_id=at(c, pair(d)), device_id_type=MESH)
    for j in range(1, nc):
        pl.semaphore_signal(barrier, inc=1, device_id=at(coef_of(j), b), device_id_type=MESH)
    for j in range(nc):
        pl.semaphore_signal(barrier, inc=1, device_id=at(coef_of(j), outer), device_id_type=MESH)
    pl.semaphore_wait(barrier, 2 * nc + len(PAIRS))

    def panel_slot(d, parity):
        return cand.at[pl.ds(PANELS_DEV * (4 + 2 * d + parity), PANELS_DEV)]

    panel_out = [
        remote(occ_hbm, panel_slot(-d, k), occ_send.at[i], occ_recv.at[i], at(c, pair(d)))
        for i, d in enumerate(PAIRS)
    ]
    for copy in panel_out:
        copy.start()
    panel_mate = remote(occ_hbm, panel_slot(0, k), mate_send.at[4], mate_recv.at[4], at(c, mate))
    panel_mate.start()

    for load in loads:
        load.wait()

    def turn(s, carry):
        at_s = pl.ds(pl.multiple_of(s * PANEL_ROWS, 128), PANEL_ROWS)
        for r in range(points // 128):
            basis_t[at_s, r * 128 : (r + 1) * 128] = basis[r * 128 : (r + 1) * 128, at_s].T
        return carry

    lax.fori_loop(0, LISTED, turn, 0)

    for i in (0, 2):
        columns[i] = coords[i].T

    def distances(left, right, out):
        mine = columns[left, pl.ds(pl.multiple_of(c * rows, 8), rows), :]
        total = None
        for axis in range(3):
            gap = mine[:, axis : axis + 1] - coords[right, axis : axis + 1, :]
            total = gap * gap if total is None else total + gap * gap
        out[...] = lax.rsqrt(total + 0.25) * (1.0 / math.sqrt(orbitals))

    distances(0, 0, kern_own)
    distances(0, 1, kern_par)
    distances(2, 0, kern_ext)

    first = (b - k - 4) * PANELS_DEV

    def invert(q, carry):
        slot = jnp.int32(LISTED)
        for s in range(LISTED):
            slot = jnp.where(listed[0, s] - first == q, s, slot)
        inverse[q] = slot
        return carry

    lax.fori_loop(0, 10 * PANELS_DEV, invert, 0)
    tiles[LISTED] = jnp.zeros_like(tiles[LISTED])

    panel_pass = [
        remote(panel_slot(d, k), panel_slot(d, k), mate_send.at[i], mate_recv.at[i], at(c, mate))
        for i, d in enumerate(PAIRS)
    ]
    for i in range(len(PAIRS)):
        arrived = len(PAIRS) - 1 - i
        panel_out[arrived].wait_recv()
        panel_pass[i].start()
    panel_mate.wait()
    for copy in panel_pass:
        copy.wait()
    for copy in panel_out:
        copy.wait_send()

    def choose(s, carry):
        chosen[pl.ds(pl.multiple_of(s * PANEL_ROWS, 128), PANEL_ROWS), :] = cand[jnp.clip(listed[0, s] - first, 0, 10 * PANELS_DEV - 1)]
        return carry

    lax.fori_loop(0, LISTED, choose, 0)

    def own_part(buffer, who, r):
        return buffer.at[who, pl.ds(r * part, part)]

    def field_copy(j, r):
        return remote(own_part(near_own, c, r), own_part(near_own, c, r), field_send.at[j, r], field_recv.at[j, r], at(coef_of(j), b))

    def pass_copy(j, r):
        who = coef_of(nc - j)
        return remote(own_part(near_own, who, r), own_part(near_par, who, r), pass_send.at[j, r], pass_recv.at[j, r], at(c, mate))

    for r in range(ROW_PARTS):
        near_own[c, r * part : (r + 1) * part] = jnp.dot(
            basis[r * part : (r + 1) * part], chosen[...], preferred_element_type=jnp.float32
        ).astype(jnp.bfloat16)

        def send(j, carry, r=r):
            field_copy(j, r).start()
            return carry

        lax.fori_loop(1, nc, send, 0)
        pass_copy(0, r).start()

    def ext_copy(j):
        to = coef_of(j)
        return remote(
            near_own.at[c, pl.ds(pl.multiple_of(to * rows, 16), rows)], ext_rows.at[c],
            ext_send.at[j], ext_recv.at[j], at(to, outer),
        )

    def send_ext_rows(j, carry):
        ext_copy(j).start()
        return carry

    lax.fori_loop(0, nc, send_ext_rows, 0)

    for r in range(ROW_PARTS):
        def forward(j, carry, r=r):
            field_copy(j, r).wait_recv()
            pass_copy(j, r).start()
            return carry

        lax.fori_loop(1, nc, forward, 0)

    def wait_ext(j, carry):
        ext_copy(j).wait()
        return carry

    lax.fori_loop(0, nc, wait_ext, 0)

    def side(ref, at_rows):
        return jnp.concatenate([ref[i, at_rows, :] for i in range(nc)], axis=1)

    def whole(ref):
        return jnp.concatenate([ref[i] for i in range(nc)], axis=1)

    my_rows = pl.ds(pl.multiple_of(c * rows, 16), rows)
    nt = (((1,), (1,)), ((), ()))
    left = side(near_own, my_rows)
    both = jnp.concatenate([left, whole(ext_rows)], axis=0)
    density = lax.dot_general(both, whole(near_own), nt, preferred_element_type=jnp.float32)
    mixed_own = (density[:rows] * kern_own[...]).astype(jnp.bfloat16)
    mixed_ext = (density[rows:] * kern_ext[...]).astype(jnp.bfloat16)
    mixed = jnp.concatenate([mixed_own, mixed_ext], axis=0)

    def ext_back(j):
        to = coef_of(j)
        return remote(send_ext.at[to], got_ext.at[c], back_send.at[j], back_recv.at[j], at(to, outer))

    def own_back(j):
        to = coef_of(j)
        return remote(send_own.at[to], got_own.at[c], own_send.at[j], own_recv.at[j], at(to, b))

    exchanged = jnp.dot(mixed, whole(near_own), preferred_element_type=jnp.float32)
    for i in range(nc):
        send_ext[i] = exchanged[rows:, i * width : (i + 1) * width].astype(jnp.bfloat16)

    def start_ext(j, carry):
        ext_back(j).start()
        return carry

    lax.fori_loop(0, nc, start_ext, 0)

    for r in range(ROW_PARTS):
        def take(j, carry, r=r):
            pass_copy(j, r).wait()
            return carry

        lax.fori_loop(0, nc, take, 0)
    density_par = lax.dot_general(left, whole(near_par), nt, preferred_element_type=jnp.float32)
    mixed_par = (density_par * kern_par[...]).astype(jnp.bfloat16)
    exchanged_own = exchanged[:rows] + jnp.dot(mixed_par, whole(near_par), preferred_element_type=jnp.float32)
    for i in range(nc):
        send_own[i] = exchanged_own[:, i * width : (i + 1) * width].astype(jnp.bfloat16)

    def start_own(j, carry):
        own_back(j).start()
        return carry

    lax.fori_loop(1, nc, start_own, 0)
    got_own[c] = send_own[c]

    def finish_field(j, carry):
        own_back(j).wait()
        for r in range(ROW_PARTS):
            field_copy(j, r).wait_send()
        return carry

    lax.fori_loop(1, nc, finish_field, 0)

    def finish_ext(j, carry):
        ext_back(j).wait()
        return carry

    lax.fori_loop(0, nc, finish_ext, 0)

    inside = jnp.logical_or(jnp.logical_and(k == 0, b > 0), jnp.logical_and(k == 1, b < ng - 1))
    for i in range(nc):
        total = got_own[i].astype(jnp.float32)
        beyond = got_ext[i].astype(jnp.float32)
        total = total + jnp.where(inside, beyond, jnp.zeros_like(beyond))
        at_i = slice(i * rows, (i + 1) * rows)
        weighted[at_i] = (total * columns[0, at_i, 3:4] * (1.0 / math.sqrt(3 * points))).astype(jnp.bfloat16)

    group = 3

    def tile(s, carry):
        value = jnp.dot(
            basis_t[pl.ds(pl.multiple_of(s * group * PANEL_ROWS, 128), group * PANEL_ROWS), :],
            weighted[...], preferred_element_type=jnp.float32,
        ) * (1.0 / math.sqrt(points))
        for i in range(group):
            tiles[s * group + i] = value[i * PANEL_ROWS : (i + 1) * PANEL_ROWS]
        return carry

    lax.fori_loop(0, LISTED // group, tile, 0)

    order = (-2, 2, -1, 1, 0)

    def comb_copy(i):
        return remote(to_mate.at[i], from_mate.at[i], comb_send.at[i], comb_recv.at[i], at(c, mate))

    for i, d in enumerate(order):
        def gather(j, carry, i=i, d=d):
            q = PANELS_DEV * (5 + 2 * d - k) + j
            to_mate[i, j] = tiles[inverse[q]].astype(jnp.bfloat16)
            return carry

        lax.fori_loop(0, PANELS_DEV, gather, 0)
        comb_copy(i).start()

    def final_copy(i):
        return remote(to_owner.at[i], from_owner.at[i], final_send.at[i], final_recv.at[i], at(c, pair(order[i])))

    for i, d in enumerate(order):
        comb_copy(i).wait()

        def combine(j, carry, i=i, d=d):
            q = PANELS_DEV * (4 + 2 * d + k) + j
            total = tiles[inverse[q]] + from_mate[i, j].astype(jnp.float32)
            if d == 0:
                out_ref[j] = total
            else:
                to_owner[i, j] = total.astype(jnp.bfloat16)
            return carry

        lax.fori_loop(0, PANELS_DEV, combine, 0)
        if d != 0:
            final_copy(i).start()
    for i in range(len(PAIRS)):
        final_copy(i).wait()
    for j in range(PANELS_DEV):
        total = out_ref[j]
        for i in range(len(PAIRS)):
            total = total + from_owner[i, j].astype(jnp.float32)
        out_ref[j] = total


def solution(mesh):
    nc, ng = mesh.shape["coef"], mesh.shape["grid"]

    def shards(basis_values, occ_coef, listed_panels, centres, point_weights):
        points, functions = basis_values.shape
        width = occ_coef.shape[1]
        rows = points // nc
        bf16, f32 = jnp.bfloat16, jnp.float32
        dma = pltpu.SemaphoreType.DMA
        panel = (PANEL_ROWS, width)
        anywhere = pl.BlockSpec(memory_space=pl.ANY)
        out = pl.pallas_call(
            functools.partial(fused, nc, ng, nc * width),
            out_shape=jax.ShapeDtypeStruct((PANELS_DEV, *panel), f32),
            in_specs=[anywhere, anywhere, pl.BlockSpec(memory_space=pltpu.SMEM), anywhere, anywhere],
            out_specs=pl.BlockSpec(memory_space=pltpu.VMEM),
            scratch_shapes=[
                pltpu.VMEM((points, functions), bf16),
                pltpu.VMEM((functions, points), bf16),
                pltpu.VMEM((10 * PANELS_DEV, *panel), bf16),
                pltpu.VMEM((functions, width), bf16),
                pltpu.VMEM((3, 8, points), f32),
                pltpu.VMEM((3, points, 8), f32),
                pltpu.SMEM((10 * PANELS_DEV,), jnp.int32),
                pltpu.VMEM((nc, points, width), bf16),
                pltpu.VMEM((nc, points, width), bf16),
                pltpu.VMEM((nc, rows, width), bf16),
                pltpu.VMEM((rows, points), f32),
                pltpu.VMEM((rows, points), f32),
                pltpu.VMEM((rows, points), f32),
                pltpu.VMEM((nc, rows, width), bf16),
                pltpu.VMEM((nc, rows, width), bf16),
                pltpu.VMEM((nc, rows, width), bf16),
                pltpu.VMEM((nc, rows, width), bf16),
                pltpu.VMEM((points, width), bf16),
                pltpu.VMEM((LISTED + 1, *panel), f32),
                pltpu.VMEM((5, PANELS_DEV, *panel), bf16),
                pltpu.VMEM((5, PANELS_DEV, *panel), bf16),
                pltpu.VMEM((4, PANELS_DEV, *panel), bf16),
                pltpu.VMEM((4, PANELS_DEV, *panel), bf16),
                dma((6,)),
                dma((4,)), dma((4,)), dma((5,)), dma((5,)),
                dma((nc, ROW_PARTS)), dma((nc, ROW_PARTS)),
                dma((nc, ROW_PARTS)), dma((nc, ROW_PARTS)),
                dma((nc,)), dma((nc,)),
                dma((nc,)), dma((nc,)), dma((nc,)), dma((nc,)),
                dma((5,)), dma((5,)), dma((4,)), dma((4,)),
            ],
            compiler_params=pltpu.CompilerParams(
                collective_id=0, has_side_effects=True, vmem_limit_bytes=56 * 2**20
            ),
        )(
            basis_values,
            occ_coef.reshape(PANELS_DEV, *panel),
            listed_panels,
            centres,
            point_weights.reshape(1, points),
        )
        return out.reshape(PANELS_DEV * PANEL_ROWS, width)

    placed = (P("grid", None), P("grid", "coef"), P("grid", None), P(), P("grid"))
    return jax.shard_map(
        shards, mesh=mesh, in_specs=placed, out_specs=P("grid", "coef"), check_vma=False
    )
```

```python
import functools
import math

import jax
import jax.numpy as jnp
from jax import lax
from jax.experimental import pallas as pl
from jax.experimental.pallas import tpu as pltpu
from jax.sharding import PartitionSpec as P

PANEL_ROWS = 128
PANELS_DEV = 5
LISTED = 21
PAIRS = (-2, -1, 1, 2)
ROW_PARTS = 2
MESH = pl.DeviceIdType.MESH


def fused(
    nc, ng, orbitals,
    basis_hbm, occ_hbm, listed, centres_hbm, weights_hbm, out_ref, from_owner,
    basis, basis_t, cand, chosen, coords, columns, inverse, near_own, near_par,
    ext_rows, kern_own, kern_par, kern_ext, send_own, send_ext, got_own, got_ext,
    weighted, tiles, to_mate, from_mate, to_owner, line,
    local_sem, occ_send, occ_recv, mate_send, mate_recv,
    field_send, field_recv, pass_send, pass_recv, ext_send, ext_recv,
    own_send, own_recv, back_send, back_recv,
    comb_send, comb_recv, final_send, final_recv,
):
    points, width = near_own.shape[1:]
    rows = points // nc
    part = points // ROW_PARTS
    c = lax.axis_index("coef")
    b = lax.axis_index("grid")
    k = lax.rem(b, 2)
    mate = b + 1 - 2 * k
    outer = b - 1 + 2 * k
    inside = jnp.logical_and(outer >= 0, outer < ng)

    def at(coef, grid):
        return {"coef": coef, "grid": grid}

    def pair(d):
        return b + 2 * d

    def exists(d):
        return pair(d) >= 0 if d < 0 else pair(d) < ng

    def remote(src, dst, send, recv, to):
        return pltpu.make_async_remote_copy(
            src_ref=src, dst_ref=dst, send_sem=send, recv_sem=recv, device_id=to, device_id_type=MESH
        )

    def coef_of(j):
        return lax.rem(c + j, nc)

    barrier = pltpu.get_barrier_semaphore()
    pl.semaphore_signal(barrier, inc=1, device_id=at(c, mate), device_id_type=MESH)
    expected = jnp.int32(nc)
    for d in PAIRS:
        @pl.when(exists(d))
        def _(d=d):
            pl.semaphore_signal(barrier, inc=1, device_id=at(c, pair(d)), device_id_type=MESH)

        expected += exists(d).astype(jnp.int32)
    for j in range(1, nc):
        pl.semaphore_signal(barrier, inc=1, device_id=at(coef_of(j), b), device_id_type=MESH)

    @pl.when(inside)
    def _():
        for j in range(nc):
            pl.semaphore_signal(barrier, inc=1, device_id=at(coef_of(j), outer), device_id_type=MESH)

    expected += inside.astype(jnp.int32) * nc

    loads = [
        pltpu.make_async_copy(basis_hbm, basis, local_sem.at[0]),
        pltpu.make_async_copy(occ_hbm, cand.at[pl.ds(PANELS_DEV * (4 + k), PANELS_DEV)], local_sem.at[1]),
        pltpu.make_async_copy(centres_hbm.at[:, pl.ds(pl.multiple_of(b * points, 128), points)], coords.at[0, pl.ds(0, 3)], local_sem.at[2]),
        pltpu.make_async_copy(centres_hbm.at[:, pl.ds(pl.multiple_of(mate * points, 128), points)], coords.at[1, pl.ds(0, 3)], local_sem.at[3]),
        pltpu.make_async_copy(weights_hbm, line, local_sem.at[4]),
    ]
    coords[...] = jnp.zeros_like(coords)
    for load in loads:
        load.start()
    load_outer = pltpu.make_async_copy(
        centres_hbm.at[:, pl.ds(pl.multiple_of(jnp.clip(outer, 0, ng - 1) * points, 128), points)], coords.at[2, pl.ds(0, 3)], local_sem.at[5]
    )
    load_outer.start()

    pl.semaphore_wait(barrier, expected)

    def panel_slot(d, parity):
        return cand.at[pl.ds(PANELS_DEV * (4 + 2 * d + parity), PANELS_DEV)]

    panel_out = [
        remote(occ_hbm, panel_slot(-d, k), occ_send.at[i], occ_recv.at[i], at(c, pair(d)))
        for i, d in enumerate(PAIRS)
    ]
    for copy, d in zip(panel_out, PAIRS):
        pl.when(exists(d))(copy.start)
    panel_mate = remote(occ_hbm, panel_slot(0, k), mate_send.at[4], mate_recv.at[4], at(c, mate))
    panel_mate.start()

    for load in loads:
        load.wait()
    load_outer.wait()
    coords[0, 3:4] = line[...].reshape(1, points)

    def turn(s, carry):
        at_s = pl.ds(pl.multiple_of(s * PANEL_ROWS, 128), PANEL_ROWS)
        for r in range(points // 128):
            basis_t[at_s, r * 128 : (r + 1) * 128] = basis[r * 128 : (r + 1) * 128, at_s].T
        return carry

    lax.fori_loop(0, LISTED, turn, 0)

    for i in (0, 2):
        columns[i] = coords[i].T

    def distances(left, right, out):
        mine = columns[left, pl.ds(pl.multiple_of(c * rows, 8), rows), :]
        total = None
        for axis in range(3):
            gap = mine[:, axis : axis + 1] - coords[right, axis : axis + 1, :]
            total = gap * gap if total is None else total + gap * gap
        out[...] = lax.rsqrt(total + 0.25) * (1.0 / math.sqrt(orbitals))

    distances(0, 0, kern_own)
    distances(0, 1, kern_par)
    distances(2, 0, kern_ext)

    first = (b - k - 4) * PANELS_DEV

    def invert(q, carry):
        slot = jnp.int32(LISTED)
        for s in range(LISTED):
            slot = jnp.where(listed[0, s] - first == q, s, slot)
        inverse[q] = slot
        return carry

    lax.fori_loop(0, 10 * PANELS_DEV, invert, 0)
    tiles[LISTED] = jnp.zeros_like(tiles[LISTED])

    panel_pass = [
        remote(panel_slot(d, k), panel_slot(d, k), mate_send.at[i], mate_recv.at[i], at(c, mate))
        for i, d in enumerate(PAIRS)
    ]
    for i, d in enumerate(PAIRS):
        @pl.when(exists(d))
        def _(i=i):
            panel_out[len(PAIRS) - 1 - i].wait_recv()
            panel_pass[i].start()

    panel_mate.wait()
    for i, d in enumerate(PAIRS):
        @pl.when(exists(d))
        def _(i=i):
            panel_pass[i].wait()
            panel_out[i].wait_send()

    def choose(s, carry):
        chosen[pl.ds(pl.multiple_of(s * PANEL_ROWS, 128), PANEL_ROWS), :] = cand[jnp.clip(listed[0, s] - first, 0, 10 * PANELS_DEV - 1)]
        return carry

    lax.fori_loop(0, LISTED, choose, 0)

    def own_part(buffer, who, r):
        return buffer.at[who, pl.ds(r * part, part)]

    def field_copy(j, r):
        return remote(own_part(near_own, c, r), own_part(near_own, c, r), field_send.at[j, r], field_recv.at[j, r], at(coef_of(j), b))

    def pass_copy(j, r):
        who = coef_of(nc - j)
        return remote(own_part(near_own, who, r), own_part(near_par, who, r), pass_send.at[j, r], pass_recv.at[j, r], at(c, mate))

    for r in range(ROW_PARTS):
        near_own[c, r * part : (r + 1) * part] = jnp.dot(
            basis[r * part : (r + 1) * part], chosen[...], preferred_element_type=jnp.float32
        ).astype(jnp.bfloat16)

        def send(j, carry, r=r):
            field_copy(j, r).start()
            return carry

        lax.fori_loop(1, nc, send, 0)
        pass_copy(0, r).start()

    def ext_copy(j):
        to = coef_of(j)
        return remote(
            near_own.at[c, pl.ds(pl.multiple_of(to * rows, 16), rows)], ext_rows.at[c],
            ext_send.at[j], ext_recv.at[j], at(to, outer),
        )

    def send_ext_rows(j, carry):
        ext_copy(j).start()
        return carry

    @pl.when(inside)
    def _():
        lax.fori_loop(0, nc, send_ext_rows, 0)

    for r in range(ROW_PARTS):
        def forward(j, carry, r=r):
            field_copy(j, r).wait_recv()
            pass_copy(j, r).start()
            return carry

        lax.fori_loop(1, nc, forward, 0)

    def wait_ext(j, carry):
        ext_copy(j).wait()
        return carry

    @pl.when(inside)
    def _():
        lax.fori_loop(0, nc, wait_ext, 0)

    def side(ref, at_rows):
        return jnp.concatenate([ref[i, at_rows, :] for i in range(nc)], axis=1)

    def whole(ref):
        return jnp.concatenate([ref[i] for i in range(nc)], axis=1)

    my_rows = pl.ds(pl.multiple_of(c * rows, 16), rows)
    nt = (((1,), (1,)), ((), ()))
    left = side(near_own, my_rows)
    both = jnp.concatenate([left, whole(ext_rows)], axis=0)
    density = lax.dot_general(both, whole(near_own), nt, preferred_element_type=jnp.float32)
    mixed_own = (density[:rows] * kern_own[...]).astype(jnp.bfloat16)
    mixed_ext = (density[rows:] * kern_ext[...]).astype(jnp.bfloat16)
    mixed = jnp.concatenate([mixed_own, mixed_ext], axis=0)

    def ext_back(j):
        to = coef_of(j)
        return remote(send_ext.at[to], got_ext.at[c], back_send.at[j], back_recv.at[j], at(to, outer))

    def own_back(j):
        to = coef_of(j)
        return remote(send_own.at[to], got_own.at[c], own_send.at[j], own_recv.at[j], at(to, b))

    exchanged = jnp.dot(mixed, whole(near_own), preferred_element_type=jnp.float32)
    for i in range(nc):
        send_ext[i] = exchanged[rows:, i * width : (i + 1) * width].astype(jnp.bfloat16)

    def start_ext(j, carry):
        ext_back(j).start()
        return carry

    @pl.when(inside)
    def _():
        lax.fori_loop(0, nc, start_ext, 0)

    for r in range(ROW_PARTS):
        def take(j, carry, r=r):
            pass_copy(j, r).wait()
            return carry

        lax.fori_loop(0, nc, take, 0)
    density_par = lax.dot_general(left, whole(near_par), nt, preferred_element_type=jnp.float32)
    mixed_par = (density_par * kern_par[...]).astype(jnp.bfloat16)
    exchanged_own = exchanged[:rows] + jnp.dot(mixed_par, whole(near_par), preferred_element_type=jnp.float32)
    for i in range(nc):
        send_own[i] = exchanged_own[:, i * width : (i + 1) * width].astype(jnp.bfloat16)

    def start_own(j, carry):
        own_back(j).start()
        return carry

    lax.fori_loop(1, nc, start_own, 0)
    got_own[c] = send_own[c]

    def finish_field(j, carry):
        own_back(j).wait()
        for r in range(ROW_PARTS):
            field_copy(j, r).wait_send()
        return carry

    lax.fori_loop(1, nc, finish_field, 0)

    def finish_ext(j, carry):
        ext_back(j).wait()
        return carry

    @pl.when(inside)
    def _():
        lax.fori_loop(0, nc, finish_ext, 0)

    for i in range(nc):
        total = got_own[i].astype(jnp.float32)
        beyond = got_ext[i].astype(jnp.float32)
        total = total + jnp.where(inside, beyond, jnp.zeros_like(beyond))
        at_i = slice(i * rows, (i + 1) * rows)
        weighted[at_i] = (total * columns[0, at_i, 3:4] * (1.0 / math.sqrt(3 * points))).astype(jnp.bfloat16)

    group = 3

    def tile(s, carry):
        value = jnp.dot(
            basis_t[pl.ds(pl.multiple_of(s * group * PANEL_ROWS, 128), group * PANEL_ROWS), :],
            weighted[...], preferred_element_type=jnp.float32,
        ) * (1.0 / math.sqrt(points))
        for i in range(group):
            tiles[s * group + i] = value[i * PANEL_ROWS : (i + 1) * PANEL_ROWS]
        return carry

    lax.fori_loop(0, LISTED // group, tile, 0)

    order = (-2, 2, -1, 1, 0)

    def comb_copy(i):
        return remote(to_mate.at[i], from_mate.at[i], comb_send.at[i], comb_recv.at[i], at(c, mate))

    for i, d in enumerate(order):
        def gather(j, carry, i=i, d=d):
            q = PANELS_DEV * (5 + 2 * d - k) + j
            to_mate[i, j] = tiles[inverse[q]].astype(jnp.bfloat16)
            return carry

        lax.fori_loop(0, PANELS_DEV, gather, 0)
        comb_copy(i).start()

    def final_copy(i):
        return remote(to_owner.at[i], from_owner.at[i], final_send.at[i], final_recv.at[i], at(c, pair(order[i])))

    for i, d in enumerate(order):
        comb_copy(i).wait()

        def combine(j, carry, i=i, d=d):
            q = PANELS_DEV * (4 + 2 * d + k) + j
            total = tiles[inverse[q]] + from_mate[i, j].astype(jnp.float32)
            if d == 0:
                out_ref[j] = total
            else:
                to_owner[i, j] = total.astype(jnp.bfloat16)
            return carry

        lax.fori_loop(0, PANELS_DEV, combine, 0)
        if d != 0:
            pl.when(exists(d))(final_copy(i).start)

    def no_sender(i):
        return pltpu.make_async_copy(from_mate.at[i], from_owner.at[i], local_sem.at[i])

    for i in range(len(PAIRS)):
        @pl.when(exists(-order[i]))
        def _(i=i):
            final_copy(i).wait_recv()

        @pl.when(jnp.logical_not(exists(-order[i])))
        def _(i=i):
            from_mate[i] = jnp.zeros_like(from_mate[i])
            no_sender(i).start()
            no_sender(i).wait()

        @pl.when(exists(order[i]))
        def _(i=i):
            final_copy(i).wait_send()


def solution(mesh):
    nc, ng = mesh.shape["coef"], mesh.shape["grid"]

    def shards(basis_values, occ_coef, listed_panels, centres, point_weights):
        points, functions = basis_values.shape
        width = occ_coef.shape[1]
        rows = points // nc
        bf16, f32 = jnp.bfloat16, jnp.float32
        dma = pltpu.SemaphoreType.DMA
        panel = (PANEL_ROWS, width)
        anywhere = pl.BlockSpec(memory_space=pl.ANY)
        own, others = pl.pallas_call(
            functools.partial(fused, nc, ng, nc * width),
            out_shape=(
                jax.ShapeDtypeStruct((PANELS_DEV, *panel), f32),
                jax.ShapeDtypeStruct((4, PANELS_DEV, *panel), bf16),
            ),
            in_specs=[anywhere, anywhere, pl.BlockSpec(memory_space=pltpu.SMEM), anywhere, anywhere],
            out_specs=(pl.BlockSpec(memory_space=pltpu.VMEM), anywhere),
            scratch_shapes=[
                pltpu.VMEM((points, functions), bf16),
                pltpu.VMEM((functions, points), bf16),
                pltpu.VMEM((10 * PANELS_DEV, *panel), bf16),
                pltpu.VMEM((functions, width), bf16),
                pltpu.VMEM((3, 8, points), f32),
                pltpu.VMEM((3, points, 8), f32),
                pltpu.SMEM((10 * PANELS_DEV,), jnp.int32),
                pltpu.VMEM((nc, points, width), bf16),
                pltpu.VMEM((nc, points, width), bf16),
                pltpu.VMEM((nc, rows, width), bf16),
                pltpu.VMEM((rows, points), f32),
                pltpu.VMEM((rows, points), f32),
                pltpu.VMEM((rows, points), f32),
                pltpu.VMEM((nc, rows, width), bf16),
                pltpu.VMEM((nc, rows, width), bf16),
                pltpu.VMEM((nc, rows, width), bf16),
                pltpu.VMEM((nc, rows, width), bf16),
                pltpu.VMEM((points, width), bf16),
                pltpu.VMEM((LISTED + 1, *panel), f32),
                pltpu.VMEM((5, PANELS_DEV, *panel), bf16),
                pltpu.VMEM((5, PANELS_DEV, *panel), bf16),
                pltpu.VMEM((4, PANELS_DEV, *panel), bf16),
                pltpu.VMEM((points,), f32),
                dma((6,)),
                dma((4,)), dma((4,)), dma((5,)), dma((5,)),
                dma((nc, ROW_PARTS)), dma((nc, ROW_PARTS)),
                dma((nc, ROW_PARTS)), dma((nc, ROW_PARTS)),
                dma((nc,)), dma((nc,)),
                dma((nc,)), dma((nc,)), dma((nc,)), dma((nc,)),
                dma((5,)), dma((5,)), dma((4,)), dma((4,)),
            ],
            compiler_params=pltpu.CompilerParams(
                collective_id=0, has_side_effects=True, vmem_limit_bytes=56 * 2**20
            ),
        )(
            basis_values,
            occ_coef.reshape(PANELS_DEV, *panel),
            listed_panels,
            centres,
            point_weights,
        )
        out = own
        for i in range(len(PAIRS)):
            out = out + others[i].astype(f32)
        return out.reshape(PANELS_DEV * PANEL_ROWS, width)

    placed = (P("grid", None), P("grid", "coef"), P("grid", None), P(), P("grid"))
    return jax.shard_map(
        shards, mesh=mesh, in_specs=placed, out_specs=P("grid", "coef"), check_vma=False
    )
```

```python
import functools
import math

import jax
import jax.numpy as jnp
from jax import lax
from jax.experimental import pallas as pl
from jax.experimental.pallas import tpu as pltpu
from jax.sharding import PartitionSpec as P

PANEL_ROWS = 128
PANELS_DEV = 5
LISTED = 21
PAIRS = (-2, -1, 1, 2)
ROW_PARTS = 2
MESH = pl.DeviceIdType.MESH


def fused(
    nc, ng, orbitals,
    basis_hbm, occ_hbm, listed, centres_hbm, weights_hbm, out_ref, from_owner,
    basis, basis_t, cand, chosen, coords, columns, inverse, near_own, near_par,
    ext_rows, density, density_par, exchanged, kern_own, kern_par, kern_ext, send_own, send_ext, got_own, got_ext,
    weighted, tiles, to_mate, from_mate, to_owner, line,
    local_sem, occ_send, occ_recv, mate_send, mate_recv,
    field_send, field_recv, pass_send, pass_recv, ext_send, ext_recv,
    own_send, own_recv, back_send, back_recv,
    comb_send, comb_recv, final_send, final_recv,
):
    points, width = near_own.shape[1:]
    rows = points // nc
    part = points // ROW_PARTS
    c = lax.axis_index("coef")
    b = lax.axis_index("grid")
    k = lax.rem(b, 2)
    mate = b + 1 - 2 * k
    outer = b - 1 + 2 * k
    inside = jnp.logical_and(outer >= 0, outer < ng)

    def at(coef, grid):
        return {"coef": coef, "grid": grid}

    def pair(d):
        return b + 2 * d

    def exists(d):
        return pair(d) >= 0 if d < 0 else pair(d) < ng

    def remote(src, dst, send, recv, to):
        return pltpu.make_async_remote_copy(
            src_ref=src, dst_ref=dst, send_sem=send, recv_sem=recv, device_id=to, device_id_type=MESH
        )

    def coef_of(j):
        return lax.rem(c + j, nc)

    barrier = pltpu.get_barrier_semaphore()
    pl.semaphore_signal(barrier, inc=1, device_id=at(c, mate), device_id_type=MESH)
    expected = jnp.int32(nc)
    for d in PAIRS:
        @pl.when(exists(d))
        def _(d=d):
            pl.semaphore_signal(barrier, inc=1, device_id=at(c, pair(d)), device_id_type=MESH)

        expected += exists(d).astype(jnp.int32)
    for j in range(1, nc):
        pl.semaphore_signal(barrier, inc=1, device_id=at(coef_of(j), b), device_id_type=MESH)

    @pl.when(inside)
    def _():
        for j in range(nc):
            pl.semaphore_signal(barrier, inc=1, device_id=at(coef_of(j), outer), device_id_type=MESH)

    expected += inside.astype(jnp.int32) * nc

    loads = [
        pltpu.make_async_copy(basis_hbm, basis, local_sem.at[0]),
        pltpu.make_async_copy(occ_hbm, cand.at[pl.ds(PANELS_DEV * (4 + k), PANELS_DEV)], local_sem.at[1]),
        pltpu.make_async_copy(centres_hbm.at[:, pl.ds(pl.multiple_of(b * points, 128), points)], coords.at[0, pl.ds(0, 3)], local_sem.at[2]),
        pltpu.make_async_copy(centres_hbm.at[:, pl.ds(pl.multiple_of(mate * points, 128), points)], coords.at[1, pl.ds(0, 3)], local_sem.at[3]),
        pltpu.make_async_copy(weights_hbm, line, local_sem.at[4]),
    ]
    coords[...] = jnp.zeros_like(coords)
    for load in loads:
        load.start()
    load_outer = pltpu.make_async_copy(
        centres_hbm.at[:, pl.ds(pl.multiple_of(jnp.clip(outer, 0, ng - 1) * points, 128), points)], coords.at[2, pl.ds(0, 3)], local_sem.at[5]
    )
    load_outer.start()

    pl.semaphore_wait(barrier, expected)

    def panel_slot(d, parity):
        return cand.at[pl.ds(PANELS_DEV * (4 + 2 * d + parity), PANELS_DEV)]

    panel_out = [
        remote(occ_hbm, panel_slot(-d, k), occ_send.at[i], occ_recv.at[i], at(c, pair(d)))
        for i, d in enumerate(PAIRS)
    ]
    for copy, d in zip(panel_out, PAIRS):
        pl.when(exists(d))(copy.start)
    panel_mate = remote(occ_hbm, panel_slot(0, k), mate_send.at[4], mate_recv.at[4], at(c, mate))
    panel_mate.start()

    for load in loads:
        load.wait()
    load_outer.wait()
    coords[0, 3:4] = line[...].reshape(1, points)

    def turn(s, carry):
        at_s = pl.ds(pl.multiple_of(s * PANEL_ROWS, 128), PANEL_ROWS)
        for r in range(points // 128):
            basis_t[at_s, r * 128 : (r + 1) * 128] = basis[r * 128 : (r + 1) * 128, at_s].T
        return carry

    lax.fori_loop(0, LISTED, turn, 0)

    for i in (0, 2):
        columns[i] = coords[i].T

    def distances(left, right, out):
        mine = columns[left, pl.ds(pl.multiple_of(c * rows, 8), rows), :]
        total = None
        for axis in range(3):
            gap = mine[:, axis : axis + 1] - coords[right, axis : axis + 1, :]
            total = gap * gap if total is None else total + gap * gap
        out[...] = lax.rsqrt(total + 0.25) * (1.0 / math.sqrt(orbitals))

    distances(0, 0, kern_own)
    distances(0, 1, kern_par)
    distances(2, 0, kern_ext)

    first = (b - k - 4) * PANELS_DEV

    def invert(q, carry):
        slot = jnp.int32(LISTED)
        for s in range(LISTED):
            slot = jnp.where(listed[0, s] - first == q, s, slot)
        inverse[q] = slot
        return carry

    lax.fori_loop(0, 10 * PANELS_DEV, invert, 0)
    tiles[LISTED] = jnp.zeros_like(tiles[LISTED])

    panel_pass = [
        remote(panel_slot(d, k), panel_slot(d, k), mate_send.at[i], mate_recv.at[i], at(c, mate))
        for i, d in enumerate(PAIRS)
    ]
    for i, d in enumerate(PAIRS):
        @pl.when(exists(d))
        def _(i=i):
            panel_out[len(PAIRS) - 1 - i].wait_recv()
            panel_pass[i].start()

    panel_mate.wait()
    for i, d in enumerate(PAIRS):
        @pl.when(exists(d))
        def _(i=i):
            panel_pass[i].wait()
            panel_out[i].wait_send()

    def choose(s, carry):
        chosen[pl.ds(pl.multiple_of(s * PANEL_ROWS, 128), PANEL_ROWS), :] = cand[jnp.clip(listed[0, s] - first, 0, 10 * PANELS_DEV - 1)]
        return carry

    lax.fori_loop(0, LISTED, choose, 0)

    across = c + 1 - 2 * lax.rem(c, 2)
    up = lax.rem(c + 2, nc)
    down = lax.rem(c + nc - 2, nc)
    far = lax.rem(c + 4, nc)

    def other(slab):
        return slab + 1 - 2 * lax.rem(slab, 2)

    arrives = (down, up, across, far, other(down), other(up), other(far), c)
    leaves = (
        ((c, up),) * 2, ((c, down),) * 2, ((c, across),) * 2, ((down, up), (up, down)),
        ((across, up),) * 2, ((across, down),) * 2, ((far, across),) * 2,
    )

    def piece(buffer, slab, r):
        return buffer.at[slab, pl.ds(r * part, part)]

    def field_copy(kind, r):
        slab, to = leaves[kind][r]
        return remote(
            piece(near_own, slab, r), piece(near_own, slab, r),
            field_send.at[kind, r], field_recv.at[kind, r], at(to, b),
        )

    def pass_copy(kind, r):
        slab = arrives[kind]
        return remote(
            piece(near_own, slab, r), piece(near_par, slab, r),
            pass_send.at[kind, r], pass_recv.at[kind, r], at(c, mate),
        )

    my_rows = pl.ds(pl.multiple_of(c * rows, 16), rows)

    def ext_copy(kind):
        slab = arrives[kind]
        return remote(near_own.at[slab, my_rows], ext_rows.at[slab], ext_send.at[kind], ext_recv.at[kind], at(c, outer))

    def arrived(kind, r, forward=()):
        field_copy(kind, r).wait_recv()
        for onward in forward:
            field_copy(onward, r).start()
        pass_copy(kind, r).start()
        if r == ROW_PARTS - 1:
            pl.when(inside)(ext_copy(kind).start)

    for r in range(ROW_PARTS):
        near_own[c, r * part : (r + 1) * part] = jnp.dot(
            basis[r * part : (r + 1) * part], chosen[...], preferred_element_type=jnp.float32
        ).astype(jnp.bfloat16)
        for kind in (2, 0, 1):
            field_copy(kind, r).start()
        pass_copy(7, r).start()
    pl.when(inside)(ext_copy(7).start)

    nt = (((1,), (1,)), ((), ()))

    def beside(ref, slabs, at_rows=slice(None)):
        return jnp.concatenate([ref[slab, at_rows, :] for slab in slabs], axis=1)

    def add_own(kinds, begin=False):
        @pl.when(inside)
        def _():
            for kind in kinds:
                ext_copy(kind).wait()

        slabs = [arrives[kind] for kind in kinds]
        both = jnp.concatenate([beside(near_own, slabs, my_rows), beside(ext_rows, slabs)], axis=0)
        term = lax.dot_general(both, beside(near_own, slabs), nt, preferred_element_type=jnp.float32)
        density[...] = term if begin else density[...] + term

    def add_par(kinds, begin=False):
        for kind in kinds:
            for r in range(ROW_PARTS):
                pass_copy(kind, r).wait()
        slabs = [arrives[kind] for kind in kinds]
        term = lax.dot_general(
            beside(near_own, slabs, my_rows), beside(near_par, slabs), nt, preferred_element_type=jnp.float32
        )
        density_par[...] = term if begin else density_par[...] + term

    arrived(2, 0, (4, 5))
    arrived(0, 0, (3,))
    arrived(1, 0)
    arrived(2, 1, (4, 5))
    arrived(1, 1, (3,))
    arrived(0, 1)
    arrived(3, 0, (6,))
    arrived(3, 1, (6,))
    add_own((7, 2), True)
    add_par((7, 2), True)
    arrived(4, 0)
    arrived(5, 0)
    arrived(4, 1)
    arrived(5, 1)
    add_own((0, 4))
    add_par((0, 4))
    add_own((1, 5))
    add_par((1, 5))
    arrived(6, 0)
    arrived(6, 1)
    add_par((3, 6))
    mixed_par = (density_par[...] * kern_par[...]).astype(jnp.bfloat16)

    def two(i):
        return (2 * i, 2 * i + 1)

    def from_par(i, carry):
        exchanged[i] = jnp.dot(mixed_par, beside(near_par, two(i)), preferred_element_type=jnp.float32)
        return carry

    lax.fori_loop(0, nc // 2, from_par, 0)
    add_own((3, 6))
    mixed = (density[...] * jnp.concatenate([kern_own[...], kern_ext[...]], axis=0)).astype(jnp.bfloat16)

    def ext_back(i, slab):
        return remote(send_ext.at[i], got_ext.at[slab], back_send.at[i], back_recv.at[slab], at(i, outer))

    def own_back(i, slab):
        return remote(send_own.at[i], got_own.at[slab], own_send.at[i], own_recv.at[slab], at(i, b))

    def from_own(i, carry):
        both = jnp.dot(mixed, beside(near_own, two(i)), preferred_element_type=jnp.float32)
        mine = both[:rows] + exchanged[i]
        for n, to in enumerate(two(i)):
            columns_n = slice(n * width, (n + 1) * width)
            send_ext[to] = both[rows:, columns_n].astype(jnp.bfloat16)
            pl.when(inside)(ext_back(to, c).start)
            send_own[to] = mine[:, columns_n].astype(jnp.bfloat16)
            pl.when(to != c)(own_back(to, c).start)
        return carry

    lax.fori_loop(0, nc // 2, from_own, 0)
    got_own[c] = send_own[c]

    def finish(i, carry):
        @pl.when(i != c)
        def _():
            own_back(i, i).wait()

        @pl.when(inside)
        def _():
            ext_back(i, i).wait()

        return carry

    lax.fori_loop(0, nc, finish, 0)
    for kind in range(len(leaves)):
        for r in range(ROW_PARTS):
            field_copy(kind, r).wait_send()

    for i in range(nc):
        total = got_own[i].astype(jnp.float32)
        beyond = got_ext[i].astype(jnp.float32)
        total = total + jnp.where(inside, beyond, jnp.zeros_like(beyond))
        at_i = slice(i * rows, (i + 1) * rows)
        weighted[at_i] = (total * columns[0, at_i, 3:4] * (1.0 / math.sqrt(3 * points))).astype(jnp.bfloat16)

    group = 7

    def tile(s, carry):
        value = jnp.dot(
            basis_t[pl.ds(pl.multiple_of(s * group * PANEL_ROWS, 128), group * PANEL_ROWS), :],
            weighted[...], preferred_element_type=jnp.float32,
        ) * (1.0 / math.sqrt(points))
        for i in range(group):
            tiles[s * group + i] = value[i * PANEL_ROWS : (i + 1) * PANEL_ROWS]
        return carry

    lax.fori_loop(0, LISTED // group, tile, 0)

    order = (-2, 2, -1, 1, 0)

    def comb_copy(i):
        return remote(to_mate.at[i], from_mate.at[i], comb_send.at[i], comb_recv.at[i], at(c, mate))

    for i, d in enumerate(order):
        def gather(j, carry, i=i, d=d):
            q = PANELS_DEV * (5 + 2 * d - k) + j
            to_mate[i, j] = tiles[inverse[q]].astype(jnp.bfloat16)
            return carry

        lax.fori_loop(0, PANELS_DEV, gather, 0)
        comb_copy(i).start()

    def final_copy(i):
        return remote(to_owner.at[i], from_owner.at[i], final_send.at[i], final_recv.at[i], at(c, pair(order[i])))

    for i, d in enumerate(order):
        comb_copy(i).wait()

        def combine(j, carry, i=i, d=d):
            q = PANELS_DEV * (4 + 2 * d + k) + j
            total = tiles[inverse[q]] + from_mate[i, j].astype(jnp.float32)
            if d == 0:
                out_ref[j] = total
            else:
                to_owner[i, j] = total.astype(jnp.bfloat16)
            return carry

        lax.fori_loop(0, PANELS_DEV, combine, 0)
        if d != 0:
            pl.when(exists(d))(final_copy(i).start)

    def no_sender(i):
        return pltpu.make_async_copy(from_mate.at[i], from_owner.at[i], local_sem.at[i])

    for i in range(len(PAIRS)):
        @pl.when(exists(-order[i]))
        def _(i=i):
            final_copy(i).wait_recv()

        @pl.when(jnp.logical_not(exists(-order[i])))
        def _(i=i):
            from_mate[i] = jnp.zeros_like(from_mate[i])
            no_sender(i).start()
            no_sender(i).wait()

        @pl.when(exists(order[i]))
        def _(i=i):
            final_copy(i).wait_send()


def solution(mesh):
    nc, ng = mesh.shape["coef"], mesh.shape["grid"]

    def shards(basis_values, occ_coef, listed_panels, centres, point_weights):
        points, functions = basis_values.shape
        width = occ_coef.shape[1]
        rows = points // nc
        bf16, f32 = jnp.bfloat16, jnp.float32
        dma = pltpu.SemaphoreType.DMA
        panel = (PANEL_ROWS, width)
        anywhere = pl.BlockSpec(memory_space=pl.ANY)
        own, others = pl.pallas_call(
            functools.partial(fused, nc, ng, nc * width),
            out_shape=(
                jax.ShapeDtypeStruct((PANELS_DEV, *panel), f32),
                jax.ShapeDtypeStruct((4, PANELS_DEV, *panel), bf16),
            ),
            in_specs=[anywhere, anywhere, pl.BlockSpec(memory_space=pltpu.SMEM), anywhere, anywhere],
            out_specs=(pl.BlockSpec(memory_space=pltpu.VMEM), anywhere),
            scratch_shapes=[
                pltpu.VMEM((points, functions), bf16),
                pltpu.VMEM((functions, points), bf16),
                pltpu.VMEM((10 * PANELS_DEV, *panel), bf16),
                pltpu.VMEM((functions, width), bf16),
                pltpu.VMEM((3, 8, points), f32),
                pltpu.VMEM((3, points, 8), f32),
                pltpu.SMEM((10 * PANELS_DEV,), jnp.int32),
                pltpu.VMEM((nc, points, width), bf16),
                pltpu.VMEM((nc, points, width), bf16),
                pltpu.VMEM((nc, rows, width), bf16),
                pltpu.VMEM((2 * rows, points), f32),
                pltpu.VMEM((rows, points), f32),
                pltpu.VMEM((nc // 2, rows, 2 * width), f32),
                pltpu.VMEM((rows, points), f32),
                pltpu.VMEM((rows, points), f32),
                pltpu.VMEM((rows, points), f32),
                pltpu.VMEM((nc, rows, width), bf16),
                pltpu.VMEM((nc, rows, width), bf16),
                pltpu.VMEM((nc, rows, width), bf16),
                pltpu.VMEM((nc, rows, width), bf16),
                pltpu.VMEM((points, width), bf16),
                pltpu.VMEM((LISTED + 1, *panel), f32),
                pltpu.VMEM((5, PANELS_DEV, *panel), bf16),
                pltpu.VMEM((5, PANELS_DEV, *panel), bf16),
                pltpu.VMEM((4, PANELS_DEV, *panel), bf16),
                pltpu.VMEM((points,), f32),
                dma((6,)),
                dma((4,)), dma((4,)), dma((5,)), dma((5,)),
                dma((nc, ROW_PARTS)), dma((nc, ROW_PARTS)),
                dma((nc, ROW_PARTS)), dma((nc, ROW_PARTS)),
                dma((nc,)), dma((nc,)),
                dma((nc,)), dma((nc,)), dma((nc,)), dma((nc,)),
                dma((5,)), dma((5,)), dma((4,)), dma((4,)),
            ],
            compiler_params=pltpu.CompilerParams(
                collective_id=0, has_side_effects=True, vmem_limit_bytes=56 * 2**20
            ),
        )(
            basis_values,
            occ_coef.reshape(PANELS_DEV, *panel),
            listed_panels,
            centres,
            point_weights,
        )
        out = own
        for i in range(len(PAIRS)):
            out = out + others[i].astype(f32)
        return out.reshape(PANELS_DEV * PANEL_ROWS, width)

    placed = (P("grid", None), P("grid", "coef"), P("grid", None), P(), P("grid"))
    return jax.shard_map(
        shards, mesh=mesh, in_specs=placed, out_specs=P("grid", "coef"), check_vma=False
    )
```

```python
import functools
import math

import jax
import jax.numpy as jnp
from jax import lax
from jax.experimental import pallas as pl
from jax.experimental.pallas import tpu as pltpu
from jax.sharding import PartitionSpec as P

PANEL_ROWS = 128
PANELS_DEV = 5
LISTED = 21
PAIRS = (-2, -1, 1, 2)
ROW_PARTS = 2
FAR = (3, 6)
MESH = pl.DeviceIdType.MESH


def fused(
    nc, ng, orbitals,
    basis_hbm, occ_hbm, listed, centres_hbm, weights_hbm, out_ref, from_owner,
    basis, basis_t, cand, chosen, coords, columns, inverse, near_own, near_par,
    ext_rows, density, density_par, exchanged, kern_own, kern_par, kern_ext, send_own, send_ext, got_own, got_ext,
    weighted, to_mate, from_mate, to_owner, line,
    local_sem, occ_send, occ_recv, mate_send, mate_recv,
    field_send, field_recv, pass_send, pass_recv, ext_send, ext_recv,
    own_send, own_recv, back_send, back_recv,
    comb_send, comb_recv, final_send, final_recv,
):
    points, width = near_own.shape[1:]
    rows = points // nc
    part = points // ROW_PARTS
    c = lax.axis_index("coef")
    b = lax.axis_index("grid")
    k = lax.rem(b, 2)
    mate = b + 1 - 2 * k
    outer = b - 1 + 2 * k
    inside = jnp.logical_and(outer >= 0, outer < ng)

    def at(coef, grid):
        return {"coef": coef, "grid": grid}

    def pair(d):
        return b + 2 * d

    def exists(d):
        return pair(d) >= 0 if d < 0 else pair(d) < ng

    def remote(src, dst, send, recv, to):
        return pltpu.make_async_remote_copy(
            src_ref=src, dst_ref=dst, send_sem=send, recv_sem=recv, device_id=to, device_id_type=MESH
        )

    def coef_of(j):
        return lax.rem(c + j, nc)

    barrier = pltpu.get_barrier_semaphore()
    pl.semaphore_signal(barrier, inc=1, device_id=at(c, mate), device_id_type=MESH)
    expected = jnp.int32(nc)
    for d in PAIRS:
        @pl.when(exists(d))
        def _(d=d):
            pl.semaphore_signal(barrier, inc=1, device_id=at(c, pair(d)), device_id_type=MESH)

        expected += exists(d).astype(jnp.int32)
    for j in range(1, nc):
        pl.semaphore_signal(barrier, inc=1, device_id=at(coef_of(j), b), device_id_type=MESH)

    @pl.when(inside)
    def _():
        for j in range(nc):
            pl.semaphore_signal(barrier, inc=1, device_id=at(coef_of(j), outer), device_id_type=MESH)

    expected += inside.astype(jnp.int32) * nc

    loads = [
        pltpu.make_async_copy(basis_hbm, basis, local_sem.at[0]),
        pltpu.make_async_copy(occ_hbm, cand.at[pl.ds(PANELS_DEV * (4 + k), PANELS_DEV)], local_sem.at[1]),
        pltpu.make_async_copy(centres_hbm.at[:, pl.ds(pl.multiple_of(b * points, 128), points)], coords.at[0, pl.ds(0, 3)], local_sem.at[2]),
        pltpu.make_async_copy(centres_hbm.at[:, pl.ds(pl.multiple_of(mate * points, 128), points)], coords.at[1, pl.ds(0, 3)], local_sem.at[3]),
        pltpu.make_async_copy(weights_hbm, line, local_sem.at[4]),
    ]
    coords[...] = jnp.zeros_like(coords)
    for load in loads:
        load.start()
    load_outer = pltpu.make_async_copy(
        centres_hbm.at[:, pl.ds(pl.multiple_of(jnp.clip(outer, 0, ng - 1) * points, 128), points)], coords.at[2, pl.ds(0, 3)], local_sem.at[5]
    )
    load_outer.start()

    pl.semaphore_wait(barrier, expected)

    def panel_slot(d, parity):
        return cand.at[pl.ds(PANELS_DEV * (4 + 2 * d + parity), PANELS_DEV)]

    panel_out = [
        remote(occ_hbm, panel_slot(-d, k), occ_send.at[i], occ_recv.at[i], at(c, pair(d)))
        for i, d in enumerate(PAIRS)
    ]
    for copy, d in zip(panel_out, PAIRS):
        pl.when(exists(d))(copy.start)
    panel_mate = remote(occ_hbm, panel_slot(0, k), mate_send.at[4], mate_recv.at[4], at(c, mate))
    panel_mate.start()

    for load in loads:
        load.wait()
    load_outer.wait()
    coords[0, 3:4] = line[...].reshape(1, points)

    def turn(s, carry):
        at_s = pl.ds(pl.multiple_of(s * PANEL_ROWS, 128), PANEL_ROWS)
        for r in range(points // 128):
            basis_t[s, :, r * 128 : (r + 1) * 128] = basis[r * 128 : (r + 1) * 128, at_s].T
        return carry

    lax.fori_loop(0, LISTED, turn, 0)

    for i in (0, 2):
        columns[i] = coords[i].T

    def distances(left, right, out):
        mine = columns[left, pl.ds(pl.multiple_of(c * rows, 8), rows), :]
        total = None
        for axis in range(3):
            gap = mine[:, axis : axis + 1] - coords[right, axis : axis + 1, :]
            total = gap * gap if total is None else total + gap * gap
        out[...] = lax.rsqrt(total + 0.25) * (1.0 / math.sqrt(orbitals))

    distances(0, 0, kern_own)
    distances(0, 1, kern_par)
    distances(2, 0, kern_ext)

    first = (b - k - 4) * PANELS_DEV

    def invert(q, carry):
        slot = jnp.int32(LISTED)
        for s in range(LISTED):
            slot = jnp.where(listed[0, s] - first == q, s, slot)
        inverse[q] = slot
        return carry

    lax.fori_loop(0, 10 * PANELS_DEV, invert, 0)
    basis_t[LISTED] = jnp.zeros_like(basis_t[LISTED])

    panel_pass = [
        remote(panel_slot(d, k), panel_slot(d, k), mate_send.at[i], mate_recv.at[i], at(c, mate))
        for i, d in enumerate(PAIRS)
    ]
    for i, d in enumerate(PAIRS):
        @pl.when(exists(d))
        def _(i=i):
            panel_out[len(PAIRS) - 1 - i].wait_recv()
            panel_pass[i].start()

    panel_mate.wait()
    for i, d in enumerate(PAIRS):
        @pl.when(exists(d))
        def _(i=i):
            panel_pass[i].wait()
            panel_out[i].wait_send()

    def choose(s, carry):
        chosen[pl.ds(pl.multiple_of(s * PANEL_ROWS, 128), PANEL_ROWS), :] = cand[jnp.clip(listed[0, s] - first, 0, 10 * PANELS_DEV - 1)]
        return carry

    lax.fori_loop(0, LISTED, choose, 0)

    across = c + 1 - 2 * lax.rem(c, 2)
    up = lax.rem(c + 2, nc)
    down = lax.rem(c + nc - 2, nc)
    far = lax.rem(c + 4, nc)

    def other(slab):
        return slab + 1 - 2 * lax.rem(slab, 2)

    arrives = (down, up, across, far, other(down), other(up), other(far), c)
    leaves = (
        ((c, up),) * 2, ((c, down),) * 2, ((c, across),) * 2, ((down, up), (up, down)),
        ((across, up),) * 2, ((across, down),) * 2, ((far, across),) * 2,
    )

    def piece(buffer, slab, r):
        return buffer.at[slab, pl.ds(r * part, part)]

    def field_copy(kind, r):
        slab, to = leaves[kind][r]
        return remote(
            piece(near_own, slab, r), piece(near_own, slab, r),
            field_send.at[kind, r], field_recv.at[kind, r], at(to, b),
        )

    def pass_copy(kind, r):
        slab = arrives[kind]
        return remote(
            piece(near_own, slab, r), piece(near_par, slab, r),
            pass_send.at[kind, r], pass_recv.at[kind, r], at(c, mate),
        )

    my_rows = pl.ds(pl.multiple_of(c * rows, 16), rows)

    def ext_copy(kind):
        if kind in FAR:
            to = arrives[kind]
            to_rows = pl.ds(pl.multiple_of(to * rows, 16), rows)
            return remote(near_own.at[c, to_rows], ext_rows.at[c], ext_send.at[kind], ext_recv.at[kind], at(to, outer))
        slab = arrives[kind]
        return remote(near_own.at[slab, my_rows], ext_rows.at[slab], ext_send.at[kind], ext_recv.at[kind], at(c, outer))

    def arrived(kind, r, forward=()):
        field_copy(kind, r).wait_recv()
        for onward in forward:
            field_copy(onward, r).start()
        pass_copy(kind, r).start()
        if r == ROW_PARTS - 1 and kind not in FAR:
            pl.when(inside)(ext_copy(kind).start)

    for r in range(ROW_PARTS):
        near_own[c, r * part : (r + 1) * part] = jnp.dot(
            basis[r * part : (r + 1) * part], chosen[...], preferred_element_type=jnp.float32
        ).astype(jnp.bfloat16)
        for kind in (2, 0, 1):
            field_copy(kind, r).start()
        pass_copy(7, r).start()
    for kind in (*FAR, 7):
        pl.when(inside)(ext_copy(kind).start)

    nt = (((1,), (1,)), ((), ()))

    def beside(ref, slabs, at_rows=slice(None)):
        return jnp.concatenate([ref[slab, at_rows, :] for slab in slabs], axis=1)

    def add_own(kinds, begin=False):
        @pl.when(inside)
        def _():
            for kind in kinds:
                ext_copy(kind).wait()

        slabs = [arrives[kind] for kind in kinds]
        both = jnp.concatenate([beside(near_own, slabs, my_rows), beside(ext_rows, slabs)], axis=0)
        term = lax.dot_general(both, beside(near_own, slabs), nt, preferred_element_type=jnp.float32)
        density[...] = term if begin else density[...] + term

    def add_par(kinds, begin=False):
        for kind in kinds:
            for r in range(ROW_PARTS):
                pass_copy(kind, r).wait()
        slabs = [arrives[kind] for kind in kinds]
        term = lax.dot_general(
            beside(near_own, slabs, my_rows), beside(near_par, slabs), nt, preferred_element_type=jnp.float32
        )
        density_par[...] = term if begin else density_par[...] + term

    arrived(0, 0, (3,))
    arrived(1, 0)
    arrived(2, 0, (4, 5))
    arrived(1, 1, (3,))
    arrived(0, 1)
    arrived(2, 1, (4, 5))
    arrived(3, 0, (6,))
    arrived(3, 1, (6,))
    add_own((7, 2), True)
    add_par((7, 2), True)
    arrived(4, 0)
    arrived(5, 0)
    arrived(4, 1)
    arrived(5, 1)
    add_own((0, 4))
    add_par((0, 4))
    add_own((1, 5))
    add_par((1, 5))
    arrived(6, 0)
    arrived(6, 1)
    add_par((3, 6))
    mixed_par = (density_par[...] * kern_par[...]).astype(jnp.bfloat16)

    def two(i):
        return (2 * i, 2 * i + 1)

    def from_par(i, carry):
        exchanged[i] = jnp.dot(mixed_par, beside(near_par, two(i)), preferred_element_type=jnp.float32)
        return carry

    lax.fori_loop(0, nc // 2, from_par, 0)
    add_own((3, 6))
    mixed = (density[...] * jnp.concatenate([kern_own[...], kern_ext[...]], axis=0)).astype(jnp.bfloat16)

    def ext_back(i, slab):
        return remote(send_ext.at[i], got_ext.at[slab], back_send.at[i], back_recv.at[slab], at(i, outer))

    def own_back(i, slab):
        return remote(send_own.at[i], got_own.at[slab], own_send.at[i], own_recv.at[slab], at(i, b))

    def from_own(i, carry):
        both = jnp.dot(mixed, beside(near_own, two(i)), preferred_element_type=jnp.float32)
        mine = both[:rows] + exchanged[i]
        for n, to in enumerate(two(i)):
            columns_n = slice(n * width, (n + 1) * width)
            send_ext[to] = both[rows:, columns_n].astype(jnp.bfloat16)
            pl.when(inside)(ext_back(to, c).start)
            send_own[to] = mine[:, columns_n].astype(jnp.bfloat16)
            pl.when(to != c)(own_back(to, c).start)
        return carry

    lax.fori_loop(0, nc // 2, from_own, 0)
    got_own[c] = send_own[c]

    def finish(i, carry):
        @pl.when(i != c)
        def _():
            own_back(i, i).wait()

        @pl.when(inside)
        def _():
            ext_back(i, i).wait()

        return carry

    lax.fori_loop(0, nc, finish, 0)
    for kind in range(len(leaves)):
        for r in range(ROW_PARTS):
            field_copy(kind, r).wait_send()

    for i in range(nc):
        total = got_own[i].astype(jnp.float32)
        beyond = got_ext[i].astype(jnp.float32)
        total = total + jnp.where(inside, beyond, jnp.zeros_like(beyond))
        at_i = slice(i * rows, (i + 1) * rows)
        weighted[at_i] = (total * columns[0, at_i, 3:4] * (1.0 / math.sqrt(3 * points))).astype(jnp.bfloat16)

    order = (-2, 2, -1, 1, 0)

    def share(d, parity):
        first_q = PANELS_DEV * (4 + 2 * d + parity)
        left = jnp.concatenate(
            [
                basis_t[inverse[first_q + j]]
                for j in range(PANELS_DEV)
            ],
            axis=0,
        )
        value = jnp.dot(left, weighted[...], preferred_element_type=jnp.float32)
        return (value * (1.0 / math.sqrt(points))).reshape(PANELS_DEV, PANEL_ROWS, width)

    def comb_copy(i):
        return remote(to_mate.at[i], from_mate.at[i], comb_send.at[i], comb_recv.at[i], at(c, mate))

    def final_copy(i):
        return remote(to_owner.at[i], from_owner.at[i], final_send.at[i], final_recv.at[i], at(c, pair(order[i])))

    def for_mate(i):
        to_mate[i] = share(order[i], 1 - k).astype(jnp.bfloat16)
        comb_copy(i).start()

    for_mate(0)
    for i, d in enumerate(order):
        out_ref[...] = share(d, k)
        if i + 1 < len(order):
            for_mate(i + 1)
        comb_copy(i).wait()
        total = out_ref[...] + from_mate[i].astype(jnp.float32)
        if d == 0:
            out_ref[...] = total
        else:
            to_owner[i] = total.astype(jnp.bfloat16)
            pl.when(exists(d))(final_copy(i).start)

    def no_sender(i):
        return pltpu.make_async_copy(from_mate.at[i], from_owner.at[i], local_sem.at[i])

    for i in range(len(PAIRS)):
        @pl.when(exists(-order[i]))
        def _(i=i):
            final_copy(i).wait_recv()

        @pl.when(jnp.logical_not(exists(-order[i])))
        def _(i=i):
            from_mate[i] = jnp.zeros_like(from_mate[i])
            no_sender(i).start()
            no_sender(i).wait()

        @pl.when(exists(order[i]))
        def _(i=i):
            final_copy(i).wait_send()


def solution(mesh):
    nc, ng = mesh.shape["coef"], mesh.shape["grid"]

    def shards(basis_values, occ_coef, listed_panels, centres, point_weights):
        points, functions = basis_values.shape
        width = occ_coef.shape[1]
        rows = points // nc
        bf16, f32 = jnp.bfloat16, jnp.float32
        dma = pltpu.SemaphoreType.DMA
        panel = (PANEL_ROWS, width)
        anywhere = pl.BlockSpec(memory_space=pl.ANY)
        own, others = pl.pallas_call(
            functools.partial(fused, nc, ng, nc * width),
            out_shape=(
                jax.ShapeDtypeStruct((PANELS_DEV, *panel), f32),
                jax.ShapeDtypeStruct((4, PANELS_DEV, *panel), bf16),
            ),
            in_specs=[anywhere, anywhere, pl.BlockSpec(memory_space=pltpu.SMEM), anywhere, anywhere],
            out_specs=(pl.BlockSpec(memory_space=pltpu.VMEM), anywhere),
            scratch_shapes=[
                pltpu.VMEM((points, functions), bf16),
                pltpu.VMEM((LISTED + 1, PANEL_ROWS, points), bf16),
                pltpu.VMEM((10 * PANELS_DEV, *panel), bf16),
                pltpu.VMEM((functions, width), bf16),
                pltpu.VMEM((3, 8, points), f32),
                pltpu.VMEM((3, points, 8), f32),
                pltpu.SMEM((10 * PANELS_DEV,), jnp.int32),
                pltpu.VMEM((nc, points, width), bf16),
                pltpu.VMEM((nc, points, width), bf16),
                pltpu.VMEM((nc, rows, width), bf16),
                pltpu.VMEM((2 * rows, points), f32),
                pltpu.VMEM((rows, points), f32),
                pltpu.VMEM((nc // 2, rows, 2 * width), f32),
                pltpu.VMEM((rows, points), f32),
                pltpu.VMEM((rows, points), f32),
                pltpu.VMEM((rows, points), f32),
                pltpu.VMEM((nc, rows, width), bf16),
                pltpu.VMEM((nc, rows, width), bf16),
                pltpu.VMEM((nc, rows, width), bf16),
                pltpu.VMEM((nc, rows, width), bf16),
                pltpu.VMEM((points, width), bf16),
                pltpu.VMEM((5, PANELS_DEV, *panel), bf16),
                pltpu.VMEM((5, PANELS_DEV, *panel), bf16),
                pltpu.VMEM((4, PANELS_DEV, *panel), bf16),
                pltpu.VMEM((points,), f32),
                dma((6,)),
                dma((4,)), dma((4,)), dma((5,)), dma((5,)),
                dma((nc, ROW_PARTS)), dma((nc, ROW_PARTS)),
                dma((nc, ROW_PARTS)), dma((nc, ROW_PARTS)),
                dma((nc,)), dma((nc,)),
                dma((nc,)), dma((nc,)), dma((nc,)), dma((nc,)),
                dma((5,)), dma((5,)), dma((4,)), dma((4,)),
            ],
            compiler_params=pltpu.CompilerParams(
                collective_id=0, has_side_effects=True, vmem_limit_bytes=56 * 2**20
            ),
        )(
            basis_values,
            occ_coef.reshape(PANELS_DEV, *panel),
            listed_panels,
            centres,
            point_weights,
        )
        out = own
        for i in range(len(PAIRS)):
            out = out + others[i].astype(f32)
        return out.reshape(PANELS_DEV * PANEL_ROWS, width)

    placed = (P("grid", None), P("grid", "coef"), P("grid", None), P(), P("grid"))
    return jax.shard_map(
        shards, mesh=mesh, in_specs=placed, out_specs=P("grid", "coef"), check_vma=False
    )
```

```python
import functools
import math

import jax
import jax.numpy as jnp
from jax import lax
from jax.experimental import pallas as pl
from jax.experimental.pallas import tpu as pltpu
from jax.sharding import PartitionSpec as P

PANEL_ROWS = 128
PANELS_DEV = 5
LISTED = 21
PAIRS = (-2, -1, 1, 2)
ROW_PARTS = 4
MESH = pl.DeviceIdType.MESH


def fused(
    nc, ng, orbitals,
    basis_hbm, occ_hbm, listed, centres_hbm, weights_hbm, out_ref,
    basis, cand, chosen, coords, columns, inverse, near_own, near_par,
    ext_rows, exchanged, kern_own, kern_par, kern_ext, send_own, send_ext, got_own, got_ext,
    weighted, tiles, to_mate, from_mate, to_owner, from_owner, line,
    local_sem, occ_send, occ_recv, mate_send, mate_recv,
    field_send, field_recv, pass_send, pass_recv, ext_send, ext_recv,
    own_send, own_recv, back_send, back_recv,
    comb_send, comb_recv, final_send, final_recv,
):
    points, width = near_own.shape[1:]
    rows = points // nc
    part = points // ROW_PARTS
    c = lax.axis_index("coef")
    b = lax.axis_index("grid")
    k = lax.rem(b, 2)
    mate = b + 1 - 2 * k
    outer = b - 1 + 2 * k
    inside = jnp.logical_and(outer >= 0, outer < ng)

    def at(coef, grid):
        return {"coef": coef, "grid": grid}

    def pair(d):
        return b + 2 * d

    def exists(d):
        return pair(d) >= 0 if d < 0 else pair(d) < ng

    def remote(src, dst, send, recv, to):
        return pltpu.make_async_remote_copy(
            src_ref=src, dst_ref=dst, send_sem=send, recv_sem=recv, device_id=to, device_id_type=MESH
        )

    def coef_of(j):
        return lax.rem(c + j, nc)

    barrier = pltpu.get_barrier_semaphore()
    pl.semaphore_signal(barrier, inc=1, device_id=at(c, mate), device_id_type=MESH)
    expected = jnp.int32(nc)
    for d in PAIRS:
        @pl.when(exists(d))
        def _(d=d):
            pl.semaphore_signal(barrier, inc=1, device_id=at(c, pair(d)), device_id_type=MESH)

        expected += exists(d).astype(jnp.int32)
    for j in range(1, nc):
        pl.semaphore_signal(barrier, inc=1, device_id=at(coef_of(j), b), device_id_type=MESH)

    @pl.when(inside)
    def _():
        for j in range(nc):
            pl.semaphore_signal(barrier, inc=1, device_id=at(coef_of(j), outer), device_id_type=MESH)

    expected += inside.astype(jnp.int32) * nc

    loads = [
        pltpu.make_async_copy(basis_hbm, basis, local_sem.at[0]),
        pltpu.make_async_copy(occ_hbm, cand.at[pl.ds(PANELS_DEV * (4 + k), PANELS_DEV)], local_sem.at[1]),
        pltpu.make_async_copy(centres_hbm.at[:, pl.ds(pl.multiple_of(b * points, 128), points)], coords.at[0, pl.ds(0, 3)], local_sem.at[2]),
        pltpu.make_async_copy(centres_hbm.at[:, pl.ds(pl.multiple_of(mate * points, 128), points)], coords.at[1, pl.ds(0, 3)], local_sem.at[3]),
        pltpu.make_async_copy(weights_hbm, line, local_sem.at[4]),
    ]
    coords[...] = jnp.zeros_like(coords)
    for load in loads:
        load.start()
    load_outer = pltpu.make_async_copy(
        centres_hbm.at[:, pl.ds(pl.multiple_of(jnp.clip(outer, 0, ng - 1) * points, 128), points)], coords.at[2, pl.ds(0, 3)], local_sem.at[5]
    )
    load_outer.start()

    pl.semaphore_wait(barrier, expected)

    def panel_slot(d, parity):
        return cand.at[pl.ds(PANELS_DEV * (4 + 2 * d + parity), PANELS_DEV)]

    panel_out = [
        remote(occ_hbm, panel_slot(-d, k), occ_send.at[i], occ_recv.at[i], at(c, pair(d)))
        for i, d in enumerate(PAIRS)
    ]
    for copy, d in zip(panel_out, PAIRS):
        pl.when(exists(d))(copy.start)
    panel_mate = remote(occ_hbm, panel_slot(0, k), mate_send.at[4], mate_recv.at[4], at(c, mate))
    panel_mate.start()

    for load in loads:
        load.wait()
    load_outer.wait()
    coords[0, 3:4] = line[...].reshape(1, points)

    for i in (0, 2):
        columns[i] = coords[i].T

    def distances(left, right, out):
        mine = columns[left, pl.ds(pl.multiple_of(c * rows, 8), rows), :]
        total = None
        for axis in range(3):
            gap = mine[:, axis : axis + 1] - coords[right, axis : axis + 1, :]
            total = gap * gap if total is None else total + gap * gap
        out[...] = lax.rsqrt(total + 0.25) * (1.0 / math.sqrt(orbitals))

    distances(0, 0, kern_own)
    distances(0, 1, kern_par)
    distances(2, 0, kern_ext)

    first = (b - k - 4) * PANELS_DEV

    def invert(q, carry):
        slot = jnp.int32(LISTED)
        for s in range(LISTED):
            slot = jnp.where(listed[0, s] - first == q, s, slot)
        inverse[q] = slot
        return carry

    lax.fori_loop(0, 10 * PANELS_DEV, invert, 0)
    tiles[LISTED] = jnp.zeros_like(tiles[LISTED])

    panel_pass = [
        remote(panel_slot(d, k), panel_slot(d, k), mate_send.at[i], mate_recv.at[i], at(c, mate))
        for i, d in enumerate(PAIRS)
    ]
    for i, d in enumerate(PAIRS):
        @pl.when(exists(d))
        def _(i=i):
            panel_out[len(PAIRS) - 1 - i].wait_recv()
            panel_pass[i].start()

    panel_mate.wait()
    for i, d in enumerate(PAIRS):
        @pl.when(exists(d))
        def _(i=i):
            panel_pass[i].wait()
            panel_out[i].wait_send()

    def choose(s, carry):
        chosen[pl.ds(pl.multiple_of(s * PANEL_ROWS, 128), PANEL_ROWS), :] = cand[jnp.clip(listed[0, s] - first, 0, 10 * PANELS_DEV - 1)]
        return carry

    lax.fori_loop(0, LISTED, choose, 0)

    across = c + 1 - 2 * lax.rem(c, 2)
    up = lax.rem(c + 2, nc)
    down = lax.rem(c + nc - 2, nc)
    far = lax.rem(c + 4, nc)

    def other(slab):
        return slab + 1 - 2 * lax.rem(slab, 2)

    arrives = (down, up, across, far, other(down), other(up), other(far), c)
    leaves = (
        (c, up), (c, down), (c, across), None, (across, up), (across, down), (far, across),
    )

    def piece(buffer, slab, r):
        return buffer.at[slab, pl.ds(r * part, part)]

    def field_copy(kind, r):
        slab, to = leaves[kind] or ((down, up) if r % 2 == 0 else (up, down))
        return remote(
            piece(near_own, slab, r), piece(near_own, slab, r),
            field_send.at[kind, r], field_recv.at[kind, r], at(to, b),
        )

    def pass_copy(kind, r):
        slab = arrives[kind]
        return remote(
            piece(near_own, slab, r), piece(near_par, slab, r),
            pass_send.at[kind, r], pass_recv.at[kind, r], at(c, mate),
        )

    my_rows = pl.ds(pl.multiple_of(c * rows, 16), rows)

    holders = (up, down, across, far, other(up), other(down), other(far), c)

    def ext_copy(kind):
        to = holders[kind]
        to_rows = pl.ds(pl.multiple_of(to * rows, 16), rows)
        return remote(near_own.at[c, to_rows], ext_rows.at[c], ext_send.at[kind], ext_recv.at[kind], at(to, outer))

    def arrived(kind, r, forward=()):
        field_copy(kind, r).wait_recv()
        for onward in forward:
            field_copy(onward, r).start()
        pass_copy(kind, r).start()

    for r in range(ROW_PARTS):
        near_own[c, r * part : (r + 1) * part] = jnp.dot(
            basis[r * part : (r + 1) * part], chosen[...], preferred_element_type=jnp.float32
        ).astype(jnp.bfloat16)
        for kind in (2, 0, 1):
            field_copy(kind, r).start()
        pass_copy(7, r).start()
    for kind in range(nc):
        pl.when(inside)(ext_copy(kind).start)

    parts = range(ROW_PARTS)
    for r in parts:
        arrived(0, r, (3,) if r % 2 == 0 else ())
        arrived(1, r, (3,) if r % 2 == 1 else ())
    for r in parts:
        arrived(2, r, (4, 5))
    for r in parts:
        arrived(3, r, (6,))
    for r in parts:
        arrived(4, r)
        arrived(5, r)
    for r in parts:
        arrived(6, r)

    nt = (((1,), (1,)), ((), ()))

    def beside(ref, slabs, at_rows=slice(None)):
        return jnp.concatenate([ref[slab, at_rows, :] for slab in slabs], axis=1)

    def two(i):
        return (2 * i, 2 * i + 1)

    @pl.when(inside)
    def _():
        for kind in range(nc):
            ext_copy(kind).wait()

    mine = beside(near_own, range(nc), my_rows)
    both = jnp.concatenate([mine, beside(ext_rows, range(nc))], axis=0)
    density = lax.dot_general(both, beside(near_own, range(nc)), nt, preferred_element_type=jnp.float32)
    mixed = (density * jnp.concatenate([kern_own[...], kern_ext[...]], axis=0)).astype(jnp.bfloat16)

    def ext_back(i, slab):
        return remote(send_ext.at[i], got_ext.at[slab], back_send.at[i], back_recv.at[slab], at(i, outer))

    def own_back(i, slab):
        return remote(send_own.at[i], got_own.at[slab], own_send.at[i], own_recv.at[slab], at(i, b))

    def from_own(i, carry):
        value = jnp.dot(mixed, beside(near_own, two(i)), preferred_element_type=jnp.float32)
        exchanged[i] = value[:rows]
        for n, to in enumerate(two(i)):
            send_ext[to] = value[rows:, n * width : (n + 1) * width].astype(jnp.bfloat16)
            pl.when(inside)(ext_back(to, c).start)
        return carry

    lax.fori_loop(0, nc // 2, from_own, 0)

    for kind in range(nc):
        for r in parts:
            pass_copy(kind, r).wait()
    density_par = lax.dot_general(
        beside(near_own, range(nc), my_rows), beside(near_par, range(nc)), nt, preferred_element_type=jnp.float32
    )
    mixed_par = (density_par * kern_par[...]).astype(jnp.bfloat16)

    def from_par(i, carry):
        value = exchanged[i] + jnp.dot(mixed_par, beside(near_par, two(i)), preferred_element_type=jnp.float32)
        for n, to in enumerate(two(i)):
            send_own[to] = value[:, n * width : (n + 1) * width].astype(jnp.bfloat16)
            pl.when(to != c)(own_back(to, c).start)
        return carry

    lax.fori_loop(0, nc // 2, from_par, 0)
    got_own[c] = send_own[c]

    def finish(i, carry):
        @pl.when(i != c)
        def _():
            own_back(i, i).wait()

        @pl.when(inside)
        def _():
            ext_back(i, i).wait()

        return carry

    lax.fori_loop(0, nc, finish, 0)
    for kind in range(len(leaves)):
        for r in range(ROW_PARTS):
            field_copy(kind, r).wait_send()

    for i in range(nc):
        total = got_own[i].astype(jnp.float32)
        beyond = got_ext[i].astype(jnp.float32)
        total = total + jnp.where(inside, beyond, jnp.zeros_like(beyond))
        at_i = slice(i * rows, (i + 1) * rows)
        weighted[at_i] = (total * columns[0, at_i, 3:4] * (1.0 / math.sqrt(3 * points))).astype(jnp.bfloat16)

    turned = jnp.concatenate([weighted[i * 128 : (i + 1) * 128, :].T for i in range(points // 128)], axis=1)
    group = 3
    for s in range(LISTED // group):
        value = jnp.dot(
            turned, basis[:, s * group * PANEL_ROWS : (s + 1) * group * PANEL_ROWS], preferred_element_type=jnp.float32
        ) * (1.0 / math.sqrt(points))
        for i in range(group):
            tiles[s * group + i] = value[:, i * PANEL_ROWS : (i + 1) * PANEL_ROWS]

    order = (-1, 1, -2, 2, 0)

    def comb_copy(i):
        return remote(to_mate.at[i], from_mate.at[i], comb_send.at[i], comb_recv.at[i], at(c, mate))

    def final_copy(i):
        return remote(to_owner.at[i], from_owner.at[i], final_send.at[i], final_recv.at[i], at(c, pair(order[i])))

    for i, d in enumerate(order):
        for j in range(PANELS_DEV):
            to_mate[i, j] = tiles[inverse[PANELS_DEV * (5 + 2 * d - k) + j]].astype(jnp.bfloat16)
        comb_copy(i).start()
    for i, d in enumerate(order):
        comb_copy(i).wait()
        for j in range(PANELS_DEV):
            total = tiles[inverse[PANELS_DEV * (4 + 2 * d + k) + j]] + from_mate[i, j].astype(jnp.float32)
            if d == 0:
                out_ref[j] = total
            else:
                to_owner[i, j] = total.astype(jnp.bfloat16)
        if d != 0:
            pl.when(exists(d))(final_copy(i).start)

    for i, d in enumerate(order[:-1]):
        sent = exists(-d)
        pl.when(sent)(final_copy(i).wait_recv)
        for j in range(PANELS_DEV):
            term = from_owner[i, j].astype(jnp.float32)
            out_ref[j] += jnp.where(sent, term, jnp.zeros_like(term))
    for j in range(PANELS_DEV):
        out_ref[j] = out_ref[j].T
    for i, d in enumerate(order[:-1]):
        pl.when(exists(d))(final_copy(i).wait_send)


def solution(mesh):
    nc, ng = mesh.shape["coef"], mesh.shape["grid"]

    def shards(basis_values, occ_coef, listed_panels, centres, point_weights):
        points, functions = basis_values.shape
        width = occ_coef.shape[1]
        rows = points // nc
        bf16, f32 = jnp.bfloat16, jnp.float32
        dma = pltpu.SemaphoreType.DMA
        panel = (PANEL_ROWS, width)
        anywhere = pl.BlockSpec(memory_space=pl.ANY)
        out = pl.pallas_call(
            functools.partial(fused, nc, ng, nc * width),
            out_shape=jax.ShapeDtypeStruct((PANELS_DEV, *panel), f32),
            in_specs=[anywhere, anywhere, pl.BlockSpec(memory_space=pltpu.SMEM), anywhere, anywhere],
            out_specs=pl.BlockSpec(memory_space=pltpu.VMEM),
            scratch_shapes=[
                pltpu.VMEM((points, functions), bf16),
                pltpu.VMEM((10 * PANELS_DEV, *panel), bf16),
                pltpu.VMEM((functions, width), bf16),
                pltpu.VMEM((3, 8, points), f32),
                pltpu.VMEM((3, points, 8), f32),
                pltpu.SMEM((10 * PANELS_DEV,), jnp.int32),
                pltpu.VMEM((nc, points, width), bf16),
                pltpu.VMEM((nc, points, width), bf16),
                pltpu.VMEM((nc, rows, width), bf16),
                pltpu.VMEM((nc // 2, rows, 2 * width), f32),
                pltpu.VMEM((rows, points), f32),
                pltpu.VMEM((rows, points), f32),
                pltpu.VMEM((rows, points), f32),
                pltpu.VMEM((nc, rows, width), bf16),
                pltpu.VMEM((nc, rows, width), bf16),
                pltpu.VMEM((nc, rows, width), bf16),
                pltpu.VMEM((nc, rows, width), bf16),
                pltpu.VMEM((points, width), bf16),
                pltpu.VMEM((LISTED + 1, *panel), f32),
                pltpu.VMEM((5, PANELS_DEV, *panel), bf16),
                pltpu.VMEM((5, PANELS_DEV, *panel), bf16),
                pltpu.VMEM((4, PANELS_DEV, *panel), bf16),
                pltpu.VMEM((4, PANELS_DEV, *panel), bf16),
                pltpu.VMEM((points,), f32),
                dma((6,)),
                dma((4,)), dma((4,)), dma((5,)), dma((5,)),
                dma((nc, ROW_PARTS)), dma((nc, ROW_PARTS)),
                dma((nc, ROW_PARTS)), dma((nc, ROW_PARTS)),
                dma((nc,)), dma((nc,)),
                dma((nc,)), dma((nc,)), dma((nc,)), dma((nc,)),
                dma((5,)), dma((5,)), dma((4,)), dma((4,)),
            ],
            compiler_params=pltpu.CompilerParams(
                collective_id=0, has_side_effects=True, vmem_limit_bytes=56 * 2**20
            ),
        )(
            basis_values,
            occ_coef.reshape(PANELS_DEV, *panel),
            listed_panels,
            centres,
            point_weights,
        )
        return out.reshape(PANELS_DEV * PANEL_ROWS, width)

    placed = (P("grid", None), P("grid", "coef"), P("grid", None), P(), P("grid"))
    return jax.shard_map(
        shards, mesh=mesh, in_specs=placed, out_specs=P("grid", "coef"), check_vma=False
    )
```

```python
import functools
import math

import jax
import jax.numpy as jnp
from jax import lax
from jax.experimental import pallas as pl
from jax.experimental.pallas import tpu as pltpu
from jax.sharding import PartitionSpec as P

PANEL_ROWS = 128
PANELS_DEV = 5
LISTED = 21
PAIRS = (-2, -1, 1, 2)
ROW_PARTS = 4
SPLIT = 2
MESH = pl.DeviceIdType.MESH


def fused(
    nc, ng, orbitals,
    basis_hbm, occ_hbm, listed, centres_hbm, weights_hbm, out_ref,
    basis, cand, chosen, coords, columns, inverse, near_own, near_par,
    ext_rows, exchanged, kern_own, kern_par, kern_ext, send_own, send_ext, got_own, got_ext,
    weighted, tiles, to_mate, from_mate, to_owner, from_owner, line,
    local_sem, occ_send, occ_recv, mate_send, mate_recv,
    field_send, field_recv, pass_send, pass_recv, ext_send, ext_recv,
    own_send, own_recv, back_send, back_recv,
    comb_send, comb_recv, final_send, final_recv,
):
    points, width = near_own.shape[1:]
    rows = points // nc
    part = points // ROW_PARTS
    c = lax.axis_index("coef")
    b = lax.axis_index("grid")
    k = lax.rem(b, 2)
    mate = b + 1 - 2 * k
    outer = b - 1 + 2 * k
    inside = jnp.logical_and(outer >= 0, outer < ng)

    def at(coef, grid):
        return {"coef": coef, "grid": grid}

    def pair(d):
        return b + 2 * d

    def exists(d):
        return jnp.logical_and(pair(d) >= 0, pair(d) < ng)

    side = 1 - 2 * lax.rem(lax.div(b, 2), 2)
    same, ahead, behind, diagonal = side, 2 * side, -2 * side, -side
    has_ahead, has_behind = exists(ahead), exists(behind)
    two_parts = ((0, SPLIT), (SPLIT, PANELS_DEV - SPLIT))

    def remote(src, dst, send, recv, to):
        return pltpu.make_async_remote_copy(
            src_ref=src, dst_ref=dst, send_sem=send, recv_sem=recv, device_id=to, device_id_type=MESH
        )

    def coef_of(j):
        return lax.rem(c + j, nc)

    barrier = pltpu.get_barrier_semaphore()
    pl.semaphore_signal(barrier, inc=1, device_id=at(c, mate), device_id_type=MESH)
    expected = jnp.int32(nc)
    for d in PAIRS:
        @pl.when(exists(d))
        def _(d=d):
            pl.semaphore_signal(barrier, inc=1, device_id=at(c, pair(d)), device_id_type=MESH)

        expected += exists(d).astype(jnp.int32)
    for j in range(1, nc):
        pl.semaphore_signal(barrier, inc=1, device_id=at(coef_of(j), b), device_id_type=MESH)

    @pl.when(inside)
    def _():
        for j in range(nc):
            pl.semaphore_signal(barrier, inc=1, device_id=at(coef_of(j), outer), device_id_type=MESH)

    expected += inside.astype(jnp.int32) * nc

    loads = [
        pltpu.make_async_copy(basis_hbm, basis, local_sem.at[0]),
        pltpu.make_async_copy(occ_hbm, cand.at[pl.ds(PANELS_DEV * (4 + k), PANELS_DEV)], local_sem.at[1]),
        pltpu.make_async_copy(centres_hbm.at[:, pl.ds(pl.multiple_of(b * points, 128), points)], coords.at[0, pl.ds(0, 3)], local_sem.at[2]),
        pltpu.make_async_copy(centres_hbm.at[:, pl.ds(pl.multiple_of(mate * points, 128), points)], coords.at[1, pl.ds(0, 3)], local_sem.at[3]),
        pltpu.make_async_copy(weights_hbm, line, local_sem.at[4]),
    ]
    coords[...] = jnp.zeros_like(coords)
    for load in loads:
        load.start()
    load_outer = pltpu.make_async_copy(
        centres_hbm.at[:, pl.ds(pl.multiple_of(jnp.clip(outer, 0, ng - 1) * points, 128), points)], coords.at[2, pl.ds(0, 3)], local_sem.at[5]
    )
    load_outer.start()

    pl.semaphore_wait(barrier, expected)

    def panel_slot(d, h):
        start, size = two_parts[h]
        return cand.at[pl.ds(PANELS_DEV * (4 + 2 * d + k) + start, size)]

    def panel_copy(role, h):
        start, size = two_parts[h]
        mine = occ_hbm.at[pl.ds(start, size)]
        src, to, dst = (
            (mine, same, -same),
            (mine, behind, ahead),
            (mine, ahead, behind),
            (panel_slot(same, h), ahead, diagonal) if h == 0 else (panel_slot(ahead, h), same, same),
        )[role]
        return remote(src, panel_slot(dst, h), occ_send.at[role, h], occ_recv.at[role, h], at(c, pair(to)))

    arrives_from = (same, ahead, behind, diagonal)

    def panel_pass(role, h):
        slot = panel_slot(arrives_from[role], h)
        return remote(slot, slot, mate_send.at[role, h], mate_recv.at[role, h], at(c, mate))

    panel_copy(0, 0).start()

    @pl.when(has_behind)
    def _():
        panel_copy(1, 1).start()
        panel_copy(1, 0).start()

    @pl.when(has_ahead)
    def _():
        panel_copy(2, 1).start()
        panel_copy(2, 0).start()

    panel_copy(0, 1).start()
    whole_slot = cand.at[pl.ds(PANELS_DEV * (4 + k), PANELS_DEV)]
    panel_mate = remote(occ_hbm, whole_slot, mate_send.at[4, 0], mate_recv.at[4, 0], at(c, mate))
    panel_mate.start()

    for load in loads:
        load.wait()
    load_outer.wait()
    coords[0, 3:4] = line[...].reshape(1, points)

    for i in (0, 2):
        columns[i] = coords[i].T

    def distances(left, right, out):
        mine = columns[left, pl.ds(pl.multiple_of(c * rows, 8), rows), :]
        total = None
        for axis in range(3):
            gap = mine[:, axis : axis + 1] - coords[right, axis : axis + 1, :]
            total = gap * gap if total is None else total + gap * gap
        out[...] = lax.rsqrt(total + 0.25) * (1.0 / math.sqrt(orbitals))

    distances(0, 0, kern_own)
    distances(0, 1, kern_par)
    distances(2, 0, kern_ext)

    first = (b - k - 4) * PANELS_DEV

    def invert(q, carry):
        slot = jnp.int32(LISTED)
        for s in range(LISTED):
            slot = jnp.where(listed[0, s] - first == q, s, slot)
        inverse[q] = slot
        return carry

    lax.fori_loop(0, 10 * PANELS_DEV, invert, 0)
    tiles[LISTED] = jnp.zeros_like(tiles[LISTED])

    def panel_here(role, h):
        panel_copy(role, h).wait_recv()
        panel_pass(role, h).start()

    panel_here(0, 0)

    @pl.when(has_ahead)
    def _():
        panel_copy(3, 0).start()
        panel_here(1, 1)
        panel_copy(3, 1).start()

    pl.when(has_behind)(lambda: panel_here(2, 1))
    panel_here(0, 1)
    pl.when(has_ahead)(lambda: panel_here(1, 0))

    @pl.when(has_behind)
    def _():
        panel_here(2, 0)
        panel_here(3, 0)
        panel_here(3, 1)

    panel_mate.wait()
    for h in range(2):
        panel_pass(0, h).wait()
        panel_copy(0, h).wait_send()

        @pl.when(has_ahead)
        def _(h=h):
            panel_pass(1, h).wait()
            panel_copy(2, h).wait_send()
            panel_copy(3, h).wait_send()

        @pl.when(has_behind)
        def _(h=h):
            panel_pass(2, h).wait()
            panel_pass(3, h).wait()
            panel_copy(1, h).wait_send()

    def choose(s, carry):
        chosen[pl.ds(pl.multiple_of(s * PANEL_ROWS, 128), PANEL_ROWS), :] = cand[jnp.clip(listed[0, s] - first, 0, 10 * PANELS_DEV - 1)]
        return carry

    lax.fori_loop(0, LISTED, choose, 0)

    across = c + 1 - 2 * lax.rem(c, 2)
    up = lax.rem(c + 2, nc)
    down = lax.rem(c + nc - 2, nc)
    far = lax.rem(c + 4, nc)

    def other(slab):
        return slab + 1 - 2 * lax.rem(slab, 2)

    arrives = (down, up, across, far, other(down), other(up), other(far), c)
    leaves = (
        (c, up), (c, down), (c, across), None, (across, up), (across, down), (far, across),
    )

    def piece(buffer, slab, r):
        return buffer.at[slab, pl.ds(r * part, part)]

    def field_copy(kind, r):
        slab, to = leaves[kind] or ((down, up) if r % 2 == 0 else (up, down))
        return remote(
            piece(near_own, slab, r), piece(near_own, slab, r),
            field_send.at[kind, r], field_recv.at[kind, r], at(to, b),
        )

    def pass_copy(kind, r):
        slab = arrives[kind]
        return remote(
            piece(near_own, slab, r), piece(near_par, slab, r),
            pass_send.at[kind, r], pass_recv.at[kind, r], at(c, mate),
        )

    my_rows = pl.ds(pl.multiple_of(c * rows, 16), rows)

    holders = (up, down, across, far, other(up), other(down), other(far), c)

    def ext_copy(kind):
        to = holders[kind]
        to_rows = pl.ds(pl.multiple_of(to * rows, 16), rows)
        return remote(near_own.at[c, to_rows], ext_rows.at[c], ext_send.at[kind], ext_recv.at[kind], at(to, outer))

    def arrived(kind, r, forward=()):
        field_copy(kind, r).wait_recv()
        for onward in forward:
            field_copy(onward, r).start()
        pass_copy(kind, r).start()

    for r in range(ROW_PARTS):
        near_own[c, r * part : (r + 1) * part] = jnp.dot(
            basis[r * part : (r + 1) * part], chosen[...], preferred_element_type=jnp.float32
        ).astype(jnp.bfloat16)
        for kind in (2, 0, 1):
            field_copy(kind, r).start()
        pass_copy(7, r).start()
    for kind in range(nc):
        pl.when(inside)(ext_copy(kind).start)

    parts = range(ROW_PARTS)
    for r in parts:
        arrived(0, r, (3,) if r % 2 == 0 else ())
        arrived(1, r, (3,) if r % 2 == 1 else ())
    for r in parts:
        arrived(2, r, (4, 5))
    for r in parts:
        arrived(3, r, (6,))
    for r in parts:
        arrived(4, r)
        arrived(5, r)
    for r in parts:
        arrived(6, r)

    nt = (((1,), (1,)), ((), ()))

    def beside(ref, slabs, at_rows=slice(None)):
        return jnp.concatenate([ref[slab, at_rows, :] for slab in slabs], axis=1)

    def two(i):
        return (2 * i, 2 * i + 1)

    @pl.when(inside)
    def _():
        for kind in range(nc):
            ext_copy(kind).wait()

    mine = beside(near_own, range(nc), my_rows)
    both = jnp.concatenate([mine, beside(ext_rows, range(nc))], axis=0)
    density = lax.dot_general(both, beside(near_own, range(nc)), nt, preferred_element_type=jnp.float32)
    mixed = (density * jnp.concatenate([kern_own[...], kern_ext[...]], axis=0)).astype(jnp.bfloat16)

    def ext_back(i, slab):
        return remote(send_ext.at[i], got_ext.at[slab], back_send.at[i], back_recv.at[slab], at(i, outer))

    def own_back(i, slab):
        return remote(send_own.at[i], got_own.at[slab], own_send.at[i], own_recv.at[slab], at(i, b))

    def from_own(i, carry):
        value = jnp.dot(mixed, beside(near_own, two(i)), preferred_element_type=jnp.float32)
        exchanged[i] = value[:rows]
        for n, to in enumerate(two(i)):
            send_ext[to] = value[rows:, n * width : (n + 1) * width].astype(jnp.bfloat16)
            pl.when(inside)(ext_back(to, c).start)
        return carry

    lax.fori_loop(0, nc // 2, from_own, 0)

    for kind in range(nc):
        for r in parts:
            pass_copy(kind, r).wait()
    density_par = lax.dot_general(
        beside(near_own, range(nc), my_rows), beside(near_par, range(nc)), nt, preferred_element_type=jnp.float32
    )
    mixed_par = (density_par * kern_par[...]).astype(jnp.bfloat16)

    def from_par(i, carry):
        value = exchanged[i] + jnp.dot(mixed_par, beside(near_par, two(i)), preferred_element_type=jnp.float32)
        for n, to in enumerate(two(i)):
            send_own[to] = value[:, n * width : (n + 1) * width].astype(jnp.bfloat16)
            pl.when(to != c)(own_back(to, c).start)
        return carry

    lax.fori_loop(0, nc // 2, from_par, 0)
    got_own[c] = send_own[c]

    def finish(i, carry):
        @pl.when(i != c)
        def _():
            own_back(i, i).wait()

        @pl.when(inside)
        def _():
            ext_back(i, i).wait()

        return carry

    lax.fori_loop(0, nc, finish, 0)
    for kind in range(len(leaves)):
        for r in range(ROW_PARTS):
            field_copy(kind, r).wait_send()

    for i in range(nc):
        total = got_own[i].astype(jnp.float32)
        beyond = got_ext[i].astype(jnp.float32)
        total = total + jnp.where(inside, beyond, jnp.zeros_like(beyond))
        at_i = slice(i * rows, (i + 1) * rows)
        weighted[at_i] = (total * columns[0, at_i, 3:4] * (1.0 / math.sqrt(3 * points))).astype(jnp.bfloat16)

    turned = jnp.concatenate([weighted[i * 128 : (i + 1) * 128, :].T for i in range(points // 128)], axis=1)
    group = 3
    for s in range(LISTED // group):
        value = jnp.dot(
            turned, basis[:, s * group * PANEL_ROWS : (s + 1) * group * PANEL_ROWS], preferred_element_type=jnp.float32
        ) * (1.0 / math.sqrt(points))
        for i in range(group):
            tiles[s * group + i] = value[:, i * PANEL_ROWS : (i + 1) * PANEL_ROWS]

    order = (diagonal, same, ahead, behind, 0)
    DIAGONAL, SAME, AHEAD, BEHIND, HERE = range(5)

    def comb_copy(i):
        return remote(to_mate.at[i], from_mate.at[i], comb_send.at[i], comb_recv.at[i], at(c, mate))

    def part_of(buffer, i, h):
        start, size = two_parts[h]
        return buffer.at[i, pl.ds(start, size)]

    def final_copy(i, h):
        to = (behind, same)[h] if i == DIAGONAL else order[i]
        return remote(
            part_of(to_owner, i, h), part_of(from_owner, i, h), final_send.at[i, h], final_recv.at[i, h], at(c, pair(to))
        )

    def combine(i, h, merge=False):
        start, size = two_parts[h]
        for j in range(start, start + size):
            total = tiles[inverse[PANELS_DEV * (4 + 2 * order[i] + k) + j]] + from_mate[i, j].astype(jnp.float32)
            if merge:
                term = from_owner[DIAGONAL, j].astype(jnp.float32)
                total = total + jnp.where(has_ahead, term, jnp.zeros_like(term))
            if i == HERE:
                out_ref[j] = total
            else:
                to_owner[i, j] = total.astype(jnp.bfloat16)

    for i, d in enumerate(order):
        for j in range(PANELS_DEV):
            to_mate[i, j] = tiles[inverse[PANELS_DEV * (5 + 2 * d - k) + j]].astype(jnp.bfloat16)
        comb_copy(i).start()

    comb_copy(DIAGONAL).wait()
    for h in (1, 0):
        combine(DIAGONAL, h)
        pl.when(has_behind)(final_copy(DIAGONAL, h).start)
    comb_copy(SAME).wait()
    combine(SAME, 1)
    final_copy(SAME, 1).start()
    comb_copy(AHEAD).wait()
    combine(AHEAD, 0)
    pl.when(has_ahead)(final_copy(AHEAD, 0).start)
    comb_copy(BEHIND).wait()
    for h in range(2):
        combine(BEHIND, h)
        pl.when(has_behind)(final_copy(BEHIND, h).start)
    comb_copy(HERE).wait()
    for h in range(2):
        combine(HERE, h)
    pl.when(has_ahead)(final_copy(DIAGONAL, 0).wait_recv)
    combine(SAME, 0, merge=True)
    final_copy(SAME, 0).start()

    @pl.when(has_ahead)
    def _():
        final_copy(DIAGONAL, 1).wait_recv()
        combine(AHEAD, 1, merge=True)
        final_copy(AHEAD, 1).start()

    for i, sent in ((BEHIND, has_ahead), (SAME, None), (AHEAD, has_behind)):
        for h in range(2):
            if sent is None:
                final_copy(i, h).wait_recv()
            else:
                pl.when(sent)(final_copy(i, h).wait_recv)
        for j in range(PANELS_DEV):
            term = from_owner[i, j].astype(jnp.float32)
            out_ref[j] += term if sent is None else jnp.where(sent, term, jnp.zeros_like(term))
    for j in range(PANELS_DEV):
        out_ref[j] = out_ref[j].T
    for h in range(2):
        final_copy(SAME, h).wait_send()
        pl.when(has_ahead)(final_copy(AHEAD, h).wait_send)

        @pl.when(has_behind)
        def _(h=h):
            final_copy(DIAGONAL, h).wait_send()
            final_copy(BEHIND, h).wait_send()


def solution(mesh):
    nc, ng = mesh.shape["coef"], mesh.shape["grid"]

    def shards(basis_values, occ_coef, listed_panels, centres, point_weights):
        points, functions = basis_values.shape
        width = occ_coef.shape[1]
        rows = points // nc
        bf16, f32 = jnp.bfloat16, jnp.float32
        dma = pltpu.SemaphoreType.DMA
        panel = (PANEL_ROWS, width)
        anywhere = pl.BlockSpec(memory_space=pl.ANY)
        out = pl.pallas_call(
            functools.partial(fused, nc, ng, nc * width),
            out_shape=jax.ShapeDtypeStruct((PANELS_DEV, *panel), f32),
            in_specs=[anywhere, anywhere, pl.BlockSpec(memory_space=pltpu.SMEM), anywhere, anywhere],
            out_specs=pl.BlockSpec(memory_space=pltpu.VMEM),
            scratch_shapes=[
                pltpu.VMEM((points, functions), bf16),
                pltpu.VMEM((10 * PANELS_DEV, *panel), bf16),
                pltpu.VMEM((functions, width), bf16),
                pltpu.VMEM((3, 8, points), f32),
                pltpu.VMEM((3, points, 8), f32),
                pltpu.SMEM((10 * PANELS_DEV,), jnp.int32),
                pltpu.VMEM((nc, points, width), bf16),
                pltpu.VMEM((nc, points, width), bf16),
                pltpu.VMEM((nc, rows, width), bf16),
                pltpu.VMEM((nc // 2, rows, 2 * width), f32),
                pltpu.VMEM((rows, points), f32),
                pltpu.VMEM((rows, points), f32),
                pltpu.VMEM((rows, points), f32),
                pltpu.VMEM((nc, rows, width), bf16),
                pltpu.VMEM((nc, rows, width), bf16),
                pltpu.VMEM((nc, rows, width), bf16),
                pltpu.VMEM((nc, rows, width), bf16),
                pltpu.VMEM((points, width), bf16),
                pltpu.VMEM((LISTED + 1, *panel), f32),
                pltpu.VMEM((5, PANELS_DEV, *panel), bf16),
                pltpu.VMEM((5, PANELS_DEV, *panel), bf16),
                pltpu.VMEM((4, PANELS_DEV, *panel), bf16),
                pltpu.VMEM((4, PANELS_DEV, *panel), bf16),
                pltpu.VMEM((points,), f32),
                dma((6,)),
                dma((4, 2)), dma((4, 2)), dma((5, 2)), dma((5, 2)),
                dma((nc, ROW_PARTS)), dma((nc, ROW_PARTS)),
                dma((nc, ROW_PARTS)), dma((nc, ROW_PARTS)),
                dma((nc,)), dma((nc,)),
                dma((nc,)), dma((nc,)), dma((nc,)), dma((nc,)),
                dma((5,)), dma((5,)), dma((4, 2)), dma((4, 2)),
            ],
            compiler_params=pltpu.CompilerParams(
                collective_id=0, has_side_effects=True, vmem_limit_bytes=56 * 2**20
            ),
        )(
            basis_values,
            occ_coef.reshape(PANELS_DEV, *panel),
            listed_panels,
            centres,
            point_weights,
        )
        return out.reshape(PANELS_DEV * PANEL_ROWS, width)

    placed = (P("grid", None), P("grid", "coef"), P("grid", None), P(), P("grid"))
    return jax.shard_map(
        shards, mesh=mesh, in_specs=placed, out_specs=P("grid", "coef"), check_vma=False
    )
```

```python
import functools
import math

import jax
import jax.numpy as jnp
from jax import lax
from jax.experimental import pallas as pl
from jax.experimental.pallas import tpu as pltpu
from jax.sharding import PartitionSpec as P

PANEL_ROWS = 128
PANELS_DEV = 5
LISTED = 21
PAIRS = (-2, -1, 1, 2)
ROW_PARTS = 4
SPLIT = 3
MESH = pl.DeviceIdType.MESH


def fused(
    nc, ng, orbitals,
    basis_hbm, occ_hbm, listed_hbm, centres_hbm, weights_hbm, out_hbm,
    listed, out_ref, basis, cand, chosen, coords, columns, inverse, near_own, near_par,
    ext_rows, exchanged, kern_own, kern_par, kern_ext, send_own, send_ext, got_own, got_ext,
    weighted, tiles, to_mate, from_mate, to_owner, from_owner, line,
    local_sem, occ_send, occ_recv, mate_send, mate_recv,
    field_send, field_recv, pass_send, pass_recv, ext_send, ext_recv,
    own_send, own_recv, back_send, back_recv,
    comb_send, comb_recv, final_send, final_recv,
):
    points, width = near_own.shape[1:]
    rows = points // nc
    part = points // ROW_PARTS
    c = lax.axis_index("coef")
    b = lax.axis_index("grid")
    k = lax.rem(b, 2)
    mate = b + 1 - 2 * k
    outer = b - 1 + 2 * k
    inside = jnp.logical_and(outer >= 0, outer < ng)

    def at(coef, grid):
        return {"coef": coef, "grid": grid}

    def pair(d):
        return b + 2 * d

    def exists(d):
        return jnp.logical_and(pair(d) >= 0, pair(d) < ng)

    side = 1 - 2 * lax.rem(lax.div(b, 2), 2)
    same, ahead, behind, diagonal = side, 2 * side, -2 * side, -side
    has_ahead, has_behind = exists(ahead), exists(behind)
    near_parts, far_parts = range(SPLIT), range(SPLIT, PANELS_DEV)
    every = range(PANELS_DEV)

    def remote(src, dst, send, recv, to):
        return pltpu.make_async_remote_copy(
            src_ref=src, dst_ref=dst, send_sem=send, recv_sem=recv, device_id=to, device_id_type=MESH
        )

    def coef_of(j):
        return lax.rem(c + j, nc)

    barrier = pltpu.get_barrier_semaphore()
    pl.semaphore_signal(barrier, inc=1, device_id=at(c, mate), device_id_type=MESH)
    expected = jnp.int32(nc)
    for d in PAIRS:
        @pl.when(exists(d))
        def _(d=d):
            pl.semaphore_signal(barrier, inc=1, device_id=at(c, pair(d)), device_id_type=MESH)

        expected += exists(d).astype(jnp.int32)
    for j in range(1, nc):
        pl.semaphore_signal(barrier, inc=1, device_id=at(coef_of(j), b), device_id_type=MESH)

    @pl.when(inside)
    def _():
        for j in range(nc):
            pl.semaphore_signal(barrier, inc=1, device_id=at(coef_of(j), outer), device_id_type=MESH)

    expected += inside.astype(jnp.int32) * nc

    loads = [
        pltpu.make_async_copy(basis_hbm, basis, local_sem.at[0]),
        pltpu.make_async_copy(occ_hbm, cand.at[pl.ds(PANELS_DEV * (4 + k), PANELS_DEV)], local_sem.at[1]),
        pltpu.make_async_copy(centres_hbm.at[:, pl.ds(pl.multiple_of(b * points, 128), points)], coords.at[0, pl.ds(0, 3)], local_sem.at[2]),
        pltpu.make_async_copy(centres_hbm.at[:, pl.ds(pl.multiple_of(mate * points, 128), points)], coords.at[1, pl.ds(0, 3)], local_sem.at[3]),
        pltpu.make_async_copy(weights_hbm, line, local_sem.at[4]),
        pltpu.make_async_copy(listed_hbm, listed, local_sem.at[6]),
    ]
    coords[...] = jnp.zeros_like(coords)
    for load in loads:
        load.start()
    load_outer = pltpu.make_async_copy(
        centres_hbm.at[:, pl.ds(pl.multiple_of(jnp.clip(outer, 0, ng - 1) * points, 128), points)], coords.at[2, pl.ds(0, 3)], local_sem.at[5]
    )
    load_outer.start()

    pl.semaphore_wait(barrier, expected)

    def panel_slot(d, h):
        return cand.at[pl.ds(PANELS_DEV * (4 + 2 * d + k) + h, 1)]

    def panel_copy(role, h):
        mine = occ_hbm.at[pl.ds(h, 1)]
        src, to, dst = (
            (mine, same, -same),
            (mine, behind, ahead),
            (mine, ahead, behind),
            (panel_slot(same, h), ahead, diagonal) if h in near_parts else (panel_slot(ahead, h), same, same),
        )[role]
        return remote(src, panel_slot(dst, h), occ_send.at[role, h], occ_recv.at[role, h], at(c, pair(to)))

    arrives_from = (same, ahead, behind, diagonal)

    def panel_pass(role, h):
        slot = panel_slot(arrives_from[role], h)
        return remote(slot, slot, mate_send.at[role, h], mate_recv.at[role, h], at(c, mate))

    for h in near_parts:
        panel_copy(0, h).start()

    @pl.when(has_behind)
    def _():
        for h in (*far_parts, *near_parts):
            panel_copy(1, h).start()

    @pl.when(has_ahead)
    def _():
        for h in (*far_parts, *near_parts):
            panel_copy(2, h).start()

    for h in far_parts:
        panel_copy(0, h).start()
    whole_slot = cand.at[pl.ds(PANELS_DEV * (4 + k), PANELS_DEV)]
    panel_mate = remote(occ_hbm, whole_slot, mate_send.at[4, 0], mate_recv.at[4, 0], at(c, mate))
    panel_mate.start()

    for load in loads:
        load.wait()
    load_outer.wait()
    coords[0, 3:4] = line[...].reshape(1, points)

    for i in (0, 2):
        columns[i] = coords[i].T

    def distances(left, right, out):
        mine = columns[left, pl.ds(pl.multiple_of(c * rows, 8), rows), :]
        total = None
        for axis in range(3):
            gap = mine[:, axis : axis + 1] - coords[right, axis : axis + 1, :]
            total = gap * gap if total is None else total + gap * gap
        out[...] = lax.rsqrt(total + 0.25) * (1.0 / math.sqrt(orbitals))

    distances(0, 0, kern_own)
    distances(0, 1, kern_par)
    distances(2, 0, kern_ext)

    first = (b - k - 4) * PANELS_DEV

    def panel_here(role, h):
        panel_copy(role, h).wait_recv()
        panel_pass(role, h).start()

    for h in near_parts:
        panel_here(0, h)
        pl.when(has_ahead)(panel_copy(3, h).start)

    @pl.when(has_ahead)
    def _():
        for h in far_parts:
            panel_here(1, h)
            panel_copy(3, h).start()

    @pl.when(has_behind)
    def _():
        for h in far_parts:
            panel_here(2, h)

    for h in far_parts:
        panel_here(0, h)

    @pl.when(has_ahead)
    def _():
        for h in near_parts:
            panel_here(1, h)

    @pl.when(has_behind)
    def _():
        for h in near_parts:
            panel_here(2, h)
        for h in every:
            panel_here(3, h)

    panel_mate.wait()
    for h in every:
        panel_pass(0, h).wait()
        panel_copy(0, h).wait_send()

    @pl.when(has_ahead)
    def _():
        for h in every:
            panel_pass(1, h).wait()
            panel_copy(2, h).wait_send()
            panel_copy(3, h).wait_send()

    @pl.when(has_behind)
    def _():
        for h in every:
            panel_pass(2, h).wait()
            panel_pass(3, h).wait()
            panel_copy(1, h).wait_send()

    def choose(s, carry):
        chosen[pl.ds(pl.multiple_of(s * PANEL_ROWS, 128), PANEL_ROWS), :] = cand[jnp.clip(listed[0, s] - first, 0, 10 * PANELS_DEV - 1)]
        return carry

    lax.fori_loop(0, LISTED, choose, 0)

    across = c + 1 - 2 * lax.rem(c, 2)
    up = lax.rem(c + 2, nc)
    down = lax.rem(c + nc - 2, nc)
    far = lax.rem(c + 4, nc)

    def other(slab):
        return slab + 1 - 2 * lax.rem(slab, 2)

    arrives = (down, up, across, far, other(down), other(up), other(far), c)
    leaves = (
        (c, up), (c, down), (c, across), None, (across, up), (across, down), (far, across),
    )

    def piece(buffer, slab, r):
        return buffer.at[slab, pl.ds(r * part, part)]

    def field_copy(kind, r):
        slab, to = leaves[kind] or ((down, up) if r % 2 == 0 else (up, down))
        return remote(
            piece(near_own, slab, r), piece(near_own, slab, r),
            field_send.at[kind, r], field_recv.at[kind, r], at(to, b),
        )

    def pass_copy(kind, r):
        slab = arrives[kind]
        return remote(
            piece(near_own, slab, r), piece(near_par, slab, r),
            pass_send.at[kind, r], pass_recv.at[kind, r], at(c, mate),
        )

    my_rows = pl.ds(pl.multiple_of(c * rows, 16), rows)

    holders = (up, down, across, far, other(up), other(down), other(far), c)

    def ext_copy(kind):
        to = holders[kind]
        to_rows = pl.ds(pl.multiple_of(to * rows, 16), rows)
        return remote(near_own.at[c, to_rows], ext_rows.at[c], ext_send.at[kind], ext_recv.at[kind], at(to, outer))

    def arrived(kind, r, forward=()):
        field_copy(kind, r).wait_recv()
        for onward in forward:
            field_copy(onward, r).start()
        pass_copy(kind, r).start()

    for r in range(ROW_PARTS):
        near_own[c, r * part : (r + 1) * part] = jnp.dot(
            basis[r * part : (r + 1) * part], chosen[...], preferred_element_type=jnp.float32
        ).astype(jnp.bfloat16)
        for kind in (0, 1, 2):
            if r >= 2:
                field_copy(kind, r - 2).wait_send()
            field_copy(kind, r).start()
        pass_copy(7, r).start()
    for kind in range(nc):
        pl.when(inside)(ext_copy(kind).start)

    def invert(q, carry):
        slot = jnp.int32(LISTED)
        for s in range(LISTED):
            slot = jnp.where(listed[0, s] - first == q, s, slot)
        inverse[q] = slot
        return carry

    lax.fori_loop(0, 10 * PANELS_DEV, invert, 0)
    tiles[LISTED] = jnp.zeros_like(tiles[LISTED])

    parts = range(ROW_PARTS)
    for r in parts:
        arrived(0, r, (3,) if r % 2 == 0 else ())
        arrived(1, r, (3,) if r % 2 == 1 else ())
    for r in parts:
        arrived(2, r, (4, 5))
    for r in parts:
        arrived(3, r, (6,))
    for r in parts:
        arrived(4, r)
        arrived(5, r)
    for r in parts:
        arrived(6, r)

    nt = (((1,), (1,)), ((), ()))

    def beside(ref, slabs, at_rows=slice(None)):
        return jnp.concatenate([ref[slab, at_rows, :] for slab in slabs], axis=1)

    def two(i):
        return (2 * i, 2 * i + 1)

    @pl.when(inside)
    def _():
        for kind in range(nc):
            ext_copy(kind).wait()

    mine = beside(near_own, range(nc), my_rows)
    both = jnp.concatenate([mine, beside(ext_rows, range(nc))], axis=0)
    density = lax.dot_general(both, beside(near_own, range(nc)), nt, preferred_element_type=jnp.float32)
    mixed = (density * jnp.concatenate([kern_own[...], kern_ext[...]], axis=0)).astype(jnp.bfloat16)

    def ext_back(i, slab):
        return remote(send_ext.at[i], got_ext.at[slab], back_send.at[i], back_recv.at[slab], at(i, outer))

    def own_back(i, slab):
        return remote(send_own.at[i], got_own.at[slab], own_send.at[i], own_recv.at[slab], at(i, b))

    def from_own(i, carry):
        value = jnp.dot(mixed, beside(near_own, two(i)), preferred_element_type=jnp.float32)
        exchanged[i] = value[:rows]
        for n, to in enumerate(two(i)):
            send_ext[to] = value[rows:, n * width : (n + 1) * width].astype(jnp.bfloat16)
            pl.when(inside)(ext_back(to, c).start)
        return carry

    lax.fori_loop(0, nc // 2, from_own, 0)

    for kind in range(nc):
        for r in parts:
            pass_copy(kind, r).wait()
    density_par = lax.dot_general(
        beside(near_own, range(nc), my_rows), beside(near_par, range(nc)), nt, preferred_element_type=jnp.float32
    )
    mixed_par = (density_par * kern_par[...]).astype(jnp.bfloat16)

    def from_par(i, carry):
        value = exchanged[i] + jnp.dot(mixed_par, beside(near_par, two(i)), preferred_element_type=jnp.float32)
        for n, to in enumerate(two(i)):
            send_own[to] = value[:, n * width : (n + 1) * width].astype(jnp.bfloat16)
            pl.when(to != c)(own_back(to, c).start)
        return carry

    lax.fori_loop(0, nc // 2, from_par, 0)
    got_own[c] = send_own[c]

    def finish(i, carry):
        @pl.when(i != c)
        def _():
            own_back(i, i).wait()

        @pl.when(inside)
        def _():
            ext_back(i, i).wait()

        return carry

    lax.fori_loop(0, nc, finish, 0)
    for kind in range(len(leaves)):
        for r in range(ROW_PARTS):
            if kind > 2 or r >= ROW_PARTS - 2:
                field_copy(kind, r).wait_send()

    for i in range(nc):
        total = got_own[i].astype(jnp.float32)
        beyond = got_ext[i].astype(jnp.float32)
        total = total + jnp.where(inside, beyond, jnp.zeros_like(beyond))
        at_i = slice(i * rows, (i + 1) * rows)
        weighted[at_i] = (total * columns[0, at_i, 3:4] * (1.0 / math.sqrt(3 * points))).astype(jnp.bfloat16)

    turned = jnp.concatenate([weighted[i * 128 : (i + 1) * 128, :].T for i in range(points // 128)], axis=1)
    group = 3
    for s in range(LISTED // group):
        value = jnp.dot(
            turned, basis[:, s * group * PANEL_ROWS : (s + 1) * group * PANEL_ROWS], preferred_element_type=jnp.float32
        ) * (1.0 / math.sqrt(points))
        for i in range(group):
            tiles[s * group + i] = value[:, i * PANEL_ROWS : (i + 1) * PANEL_ROWS]

    order = (diagonal, same, ahead, behind, 0)
    DIAGONAL, SAME, AHEAD, BEHIND, HERE = range(5)

    def comb_copy(i):
        return remote(to_mate.at[i], from_mate.at[i], comb_send.at[i], comb_recv.at[i], at(c, mate))

    def part_of(buffer, i, h):
        return buffer.at[i, pl.ds(h, 1)]

    def final_copy(i, h):
        to = (behind if h in near_parts else same) if i == DIAGONAL else order[i]
        return remote(
            part_of(to_owner, i, h), part_of(from_owner, i, h), final_send.at[i, h], final_recv.at[i, h], at(c, pair(to))
        )

    def combine(i, h, merge=False):
        total = tiles[inverse[PANELS_DEV * (4 + 2 * order[i] + k) + h]] + from_mate[i, h].astype(jnp.float32)
        if merge:
            term = from_owner[DIAGONAL, h].astype(jnp.float32)
            total = total + jnp.where(has_ahead, term, jnp.zeros_like(term))
        if i == HERE:
            out_ref[h] = total
        else:
            to_owner[i, h] = total.astype(jnp.bfloat16)

    for i, d in enumerate(order):
        for j in range(PANELS_DEV):
            to_mate[i, j] = tiles[inverse[PANELS_DEV * (5 + 2 * d - k) + j]].astype(jnp.bfloat16)
        comb_copy(i).start()

    comb_copy(DIAGONAL).wait()
    for h in (3, 0, 4, 1, 2):
        combine(DIAGONAL, h)
        pl.when(has_behind)(final_copy(DIAGONAL, h).start)
    comb_copy(SAME).wait()
    for h in far_parts:
        combine(SAME, h)
        final_copy(SAME, h).start()
    comb_copy(AHEAD).wait()
    for h in near_parts:
        combine(AHEAD, h)
        pl.when(has_ahead)(final_copy(AHEAD, h).start)
    comb_copy(BEHIND).wait()
    for h in every:
        combine(BEHIND, h)
        pl.when(has_behind)(final_copy(BEHIND, h).start)
    comb_copy(HERE).wait()
    for h in every:
        combine(HERE, h)
    for h in near_parts:
        pl.when(has_ahead)(final_copy(DIAGONAL, h).wait_recv)
        combine(SAME, h, merge=True)
        final_copy(SAME, h).start()

    @pl.when(has_ahead)
    def _():
        for h in far_parts:
            final_copy(DIAGONAL, h).wait_recv()
            combine(AHEAD, h, merge=True)
            final_copy(AHEAD, h).start()

    for i, sent in ((BEHIND, has_ahead), (SAME, None), (AHEAD, has_behind)):
        for h in every:
            if sent is None:
                final_copy(i, h).wait_recv()
            else:
                pl.when(sent)(final_copy(i, h).wait_recv)
        for j in range(PANELS_DEV):
            term = from_owner[i, j].astype(jnp.float32)
            out_ref[j] += term if sent is None else jnp.where(sent, term, jnp.zeros_like(term))
    results = [pltpu.make_async_copy(out_ref.at[j], out_hbm.at[j], local_sem.at[j]) for j in range(PANELS_DEV)]
    for j, result in enumerate(results):
        out_ref[j] = out_ref[j].T
        result.start()
    for h in every:
        final_copy(SAME, h).wait_send()
        pl.when(has_ahead)(final_copy(AHEAD, h).wait_send)

        @pl.when(has_behind)
        def _(h=h):
            final_copy(DIAGONAL, h).wait_send()
            final_copy(BEHIND, h).wait_send()

    for result in results:
        result.wait()


def solution(mesh):
    nc, ng = mesh.shape["coef"], mesh.shape["grid"]

    def shards(basis_values, occ_coef, listed_panels, centres, point_weights):
        points, functions = basis_values.shape
        width = occ_coef.shape[1]
        rows = points // nc
        bf16, f32 = jnp.bfloat16, jnp.float32
        dma = pltpu.SemaphoreType.DMA
        panel = (PANEL_ROWS, width)
        anywhere = pl.BlockSpec(memory_space=pl.ANY)
        out = pl.pallas_call(
            functools.partial(fused, nc, ng, nc * width),
            out_shape=jax.ShapeDtypeStruct((PANELS_DEV, *panel), f32),
            in_specs=[anywhere] * 5,
            out_specs=anywhere,
            scratch_shapes=[
                pltpu.SMEM((1, LISTED), jnp.int32),
                pltpu.VMEM((PANELS_DEV, *panel), f32),
                pltpu.VMEM((points, functions), bf16),
                pltpu.VMEM((10 * PANELS_DEV, *panel), bf16),
                pltpu.VMEM((functions, width), bf16),
                pltpu.VMEM((3, 8, points), f32),
                pltpu.VMEM((3, points, 8), f32),
                pltpu.SMEM((10 * PANELS_DEV,), jnp.int32),
                pltpu.VMEM((nc, points, width), bf16),
                pltpu.VMEM((nc, points, width), bf16),
                pltpu.VMEM((nc, rows, width), bf16),
                pltpu.VMEM((nc // 2, rows, 2 * width), f32),
                pltpu.VMEM((rows, points), f32),
                pltpu.VMEM((rows, points), f32),
                pltpu.VMEM((rows, points), f32),
                pltpu.VMEM((nc, rows, width), bf16),
                pltpu.VMEM((nc, rows, width), bf16),
                pltpu.VMEM((nc, rows, width), bf16),
                pltpu.VMEM((nc, rows, width), bf16),
                pltpu.VMEM((points, width), bf16),
                pltpu.VMEM((LISTED + 1, *panel), f32),
                pltpu.VMEM((5, PANELS_DEV, *panel), bf16),
                pltpu.VMEM((5, PANELS_DEV, *panel), bf16),
                pltpu.VMEM((4, PANELS_DEV, *panel), bf16),
                pltpu.VMEM((4, PANELS_DEV, *panel), bf16),
                pltpu.VMEM((points,), f32),
                dma((8,)),
                dma((4, PANELS_DEV)), dma((4, PANELS_DEV)), dma((5, PANELS_DEV)), dma((5, PANELS_DEV)),
                dma((nc, ROW_PARTS)), dma((nc, ROW_PARTS)),
                dma((nc, ROW_PARTS)), dma((nc, ROW_PARTS)),
                dma((nc,)), dma((nc,)),
                dma((nc,)), dma((nc,)), dma((nc,)), dma((nc,)),
                dma((5,)), dma((5,)), dma((4, PANELS_DEV)), dma((4, PANELS_DEV)),
            ],
            compiler_params=pltpu.CompilerParams(
                collective_id=0, has_side_effects=True, vmem_limit_bytes=56 * 2**20
            ),
        )(
            basis_values,
            occ_coef.reshape(PANELS_DEV, *panel),
            listed_panels,
            centres,
            point_weights,
        )
        return out.reshape(PANELS_DEV * PANEL_ROWS, width)

    placed = (P("grid", None), P("grid", "coef"), P("grid", None), P(), P("grid"))
    return jax.shard_map(
        shards, mesh=mesh, in_specs=placed, out_specs=P("grid", "coef"), check_vma=False
    )
```

```python
import functools
import math

import jax
import jax.numpy as jnp
from jax import lax
from jax.experimental import pallas as pl
from jax.experimental.pallas import tpu as pltpu
from jax.sharding import PartitionSpec as P

PANEL_ROWS = 128
PANELS_DEV = 5
LISTED = 21
PAIRS = (-2, -1, 1, 2)
ROW_PARTS = 4
SPLIT = 3
MESH = pl.DeviceIdType.MESH


def fused(
    nc, ng, orbitals,
    basis_hbm, occ_hbm, listed_hbm, centres_hbm, weights_hbm, out_hbm,
    listed, out_ref, basis, cand, chosen, coords, columns, inverse, near_own, near_par,
    ext_rows, exchanged, kern_own, kern_par, kern_ext, send_own, send_ext, got_own, got_ext,
    weighted, tiles, to_mate, from_mate, to_owner, from_owner, line,
    local_sem, occ_send, occ_recv, mate_send, mate_recv,
    field_send, field_recv, pass_send, pass_recv, ext_send, ext_recv,
    own_send, own_recv, back_send, back_recv,
    comb_send, comb_recv, final_send, final_recv,
):
    points, width = near_own.shape[1:]
    rows = points // nc
    part = points // ROW_PARTS
    c = lax.axis_index("coef")
    b = lax.axis_index("grid")
    k = lax.rem(b, 2)
    mate = b + 1 - 2 * k
    outer = b - 1 + 2 * k
    inside = jnp.logical_and(outer >= 0, outer < ng)

    def at(coef, grid):
        return {"coef": coef, "grid": grid}

    def pair(d):
        return b + 2 * d

    def exists(d):
        return jnp.logical_and(pair(d) >= 0, pair(d) < ng)

    side = 1 - 2 * lax.rem(lax.div(b, 2), 2)
    same, ahead, behind, diagonal = side, 2 * side, -2 * side, -side
    has_ahead, has_behind = exists(ahead), exists(behind)
    near_parts, far_parts = range(SPLIT), range(SPLIT, PANELS_DEV)
    every = range(PANELS_DEV)

    def remote(src, dst, send, recv, to):
        return pltpu.make_async_remote_copy(
            src_ref=src, dst_ref=dst, send_sem=send, recv_sem=recv, device_id=to, device_id_type=MESH
        )

    def coef_of(j):
        return lax.rem(c + j, nc)

    barrier = pltpu.get_barrier_semaphore()
    pl.semaphore_signal(barrier, inc=1, device_id=at(c, mate), device_id_type=MESH)
    expected = jnp.int32(nc)
    for d in PAIRS:
        @pl.when(exists(d))
        def _(d=d):
            pl.semaphore_signal(barrier, inc=1, device_id=at(c, pair(d)), device_id_type=MESH)

        expected += exists(d).astype(jnp.int32)
    for j in range(1, nc):
        pl.semaphore_signal(barrier, inc=1, device_id=at(coef_of(j), b), device_id_type=MESH)

    @pl.when(inside)
    def _():
        for j in range(nc):
            pl.semaphore_signal(barrier, inc=1, device_id=at(coef_of(j), outer), device_id_type=MESH)

    expected += inside.astype(jnp.int32) * nc

    loads = [
        pltpu.make_async_copy(basis_hbm, basis, local_sem.at[0]),
        pltpu.make_async_copy(occ_hbm, cand.at[pl.ds(PANELS_DEV * (4 + k), PANELS_DEV)], local_sem.at[1]),
        pltpu.make_async_copy(centres_hbm.at[:, pl.ds(pl.multiple_of(b * points, 128), points)], coords.at[0, pl.ds(0, 3)], local_sem.at[2]),
        pltpu.make_async_copy(centres_hbm.at[:, pl.ds(pl.multiple_of(mate * points, 128), points)], coords.at[1, pl.ds(0, 3)], local_sem.at[3]),
        pltpu.make_async_copy(weights_hbm, line, local_sem.at[4]),
        pltpu.make_async_copy(listed_hbm, listed, local_sem.at[6]),
    ]
    coords[...] = jnp.zeros_like(coords)
    for load in loads:
        load.start()
    load_outer = pltpu.make_async_copy(
        centres_hbm.at[:, pl.ds(pl.multiple_of(jnp.clip(outer, 0, ng - 1) * points, 128), points)], coords.at[2, pl.ds(0, 3)], local_sem.at[5]
    )
    load_outer.start()

    pl.semaphore_wait(barrier, expected)

    def panel_slot(d, h):
        return cand.at[pl.ds(PANELS_DEV * (4 + 2 * d + k) + h, 1)]

    def panel_copy(role, h):
        mine = occ_hbm.at[pl.ds(h, 1)]
        src, to, dst = (
            (mine, same, -same),
            (mine, behind, ahead),
            (mine, ahead, behind),
            (panel_slot(same, h), ahead, diagonal) if h in near_parts else (panel_slot(ahead, h), same, same),
        )[role]
        return remote(src, panel_slot(dst, h), occ_send.at[role, h], occ_recv.at[role, h], at(c, pair(to)))

    arrives_from = (same, ahead, behind, diagonal)

    def panel_pass(role, h):
        slot = panel_slot(arrives_from[role], h)
        return remote(slot, slot, mate_send.at[role, h], mate_recv.at[role, h], at(c, mate))

    for h in near_parts:
        panel_copy(0, h).start()

    @pl.when(has_behind)
    def _():
        for h in (*far_parts, *near_parts):
            panel_copy(1, h).start()

    @pl.when(has_ahead)
    def _():
        for h in (*far_parts, *near_parts):
            panel_copy(2, h).start()

    for h in far_parts:
        panel_copy(0, h).start()
    whole_slot = cand.at[pl.ds(PANELS_DEV * (4 + k), PANELS_DEV)]
    panel_mate = remote(occ_hbm, whole_slot, mate_send.at[4, 0], mate_recv.at[4, 0], at(c, mate))
    panel_mate.start()

    for load in loads:
        load.wait()
    load_outer.wait()
    coords[0, 3:4] = line[...].reshape(1, points)

    for i in (0, 2):
        columns[i] = coords[i].T

    def distances(left, right, out):
        mine = columns[left, pl.ds(pl.multiple_of(c * rows, 8), rows), :]
        total = None
        for axis in range(3):
            gap = mine[:, axis : axis + 1] - coords[right, axis : axis + 1, :]
            total = gap * gap if total is None else total + gap * gap
        out[...] = lax.rsqrt(total + 0.25) * (1.0 / math.sqrt(orbitals))

    distances(0, 0, kern_own)
    distances(0, 1, kern_par)
    distances(2, 0, kern_ext)

    first = (b - k - 4) * PANELS_DEV

    def panel_here(role, h):
        panel_copy(role, h).wait_recv()
        panel_pass(role, h).start()

    for h in near_parts:
        panel_here(0, h)
        pl.when(has_ahead)(panel_copy(3, h).start)

    @pl.when(has_ahead)
    def _():
        for h in far_parts:
            panel_here(1, h)
            panel_copy(3, h).start()

    @pl.when(has_behind)
    def _():
        for h in far_parts:
            panel_here(2, h)

    for h in far_parts:
        panel_here(0, h)

    @pl.when(has_ahead)
    def _():
        for h in near_parts:
            panel_here(1, h)

    @pl.when(has_behind)
    def _():
        for h in near_parts:
            panel_here(2, h)
        for h in every:
            panel_here(3, h)

    panel_mate.wait()
    for h in every:
        panel_pass(0, h).wait()
        panel_copy(0, h).wait_send()

    @pl.when(has_ahead)
    def _():
        for h in every:
            panel_pass(1, h).wait()
            panel_copy(2, h).wait_send()
            panel_copy(3, h).wait_send()

    @pl.when(has_behind)
    def _():
        for h in every:
            panel_pass(2, h).wait()
            panel_pass(3, h).wait()
            panel_copy(1, h).wait_send()

    def choose(s, carry):
        chosen[pl.ds(pl.multiple_of(s * PANEL_ROWS, 128), PANEL_ROWS), :] = cand[jnp.clip(listed[0, s] - first, 0, 10 * PANELS_DEV - 1)]
        return carry

    lax.fori_loop(0, LISTED, choose, 0)

    across = c + 1 - 2 * lax.rem(c, 2)
    up = lax.rem(c + 2, nc)
    down = lax.rem(c + nc - 2, nc)
    far = lax.rem(c + 4, nc)

    def other(slab):
        return slab + 1 - 2 * lax.rem(slab, 2)

    arrives = (down, up, across, far, other(down), other(up), other(far), c)
    leaves = (
        (c, up), (c, down), (c, across), None, (across, up), (across, down), (far, across),
    )

    def piece(buffer, slab, r):
        return buffer.at[slab, pl.ds(r * part, part)]

    def field_copy(kind, r):
        slab, to = leaves[kind] or ((down, up) if r % 2 == 0 else (up, down))
        return remote(
            piece(near_own, slab, r), piece(near_own, slab, r),
            field_send.at[kind, r], field_recv.at[kind, r], at(to, b),
        )

    def pass_copy(kind, r):
        slab = arrives[kind]
        return remote(
            piece(near_own, slab, r), piece(near_par, slab, r),
            pass_send.at[kind, r], pass_recv.at[kind, r], at(c, mate),
        )

    my_rows = pl.ds(pl.multiple_of(c * rows, 16), rows)

    holders = (up, down, across, far, other(up), other(down), other(far), c)

    def ext_copy(kind):
        to = holders[kind]
        to_rows = pl.ds(pl.multiple_of(to * rows, 16), rows)
        return remote(near_own.at[c, to_rows], ext_rows.at[c], ext_send.at[kind], ext_recv.at[kind], at(to, outer))

    def arrived(kind, r, forward=()):
        field_copy(kind, r).wait_recv()
        for onward in forward:
            field_copy(onward, r).start()
        pass_copy(kind, r).start()

    for r in range(ROW_PARTS):
        near_own[c, r * part : (r + 1) * part] = jnp.dot(
            basis[r * part : (r + 1) * part], chosen[...], preferred_element_type=jnp.float32
        ).astype(jnp.bfloat16)
        for kind in (0, 1, 2):
            if r >= 2:
                field_copy(kind, r - 2).wait_send()
            field_copy(kind, r).start()
        pass_copy(7, r).start()
    for kind in range(nc):
        pl.when(inside)(ext_copy(kind).start)

    def invert(q, carry):
        slot = jnp.int32(LISTED)
        for s in range(LISTED):
            slot = jnp.where(listed[0, s] - first == q, s, slot)
        inverse[q] = slot
        return carry

    lax.fori_loop(0, 10 * PANELS_DEV, invert, 0)
    tiles[LISTED] = jnp.zeros_like(tiles[LISTED])

    parts = range(ROW_PARTS)
    for r in parts:
        arrived(0, r, (3,) if r % 2 == 0 else ())
        arrived(1, r, (3,) if r % 2 == 1 else ())
    for r in parts:
        arrived(2, r, (4, 5))
    for r in parts:
        arrived(3, r, (6,))
    for r in parts:
        arrived(4, r)
        arrived(5, r)
    for r in parts:
        arrived(6, r)

    nt = (((1,), (1,)), ((), ()))

    def beside(ref, slabs, at_rows=slice(None)):
        return jnp.concatenate([ref[slab, at_rows, :] for slab in slabs], axis=1)

    def two(n):
        place = lax.rem(lax.div(c, 2) + jnp.where(n < 2, n + 2, 3 - n), nc // 2)
        return (2 * place, 2 * place + 1)

    @pl.when(inside)
    def _():
        for kind in range(nc):
            ext_copy(kind).wait()

    mine = beside(near_own, range(nc), my_rows)
    both = jnp.concatenate([mine, beside(ext_rows, range(nc))], axis=0)
    density = lax.dot_general(both, beside(near_own, range(nc)), nt, preferred_element_type=jnp.float32)
    mixed = (density * jnp.concatenate([kern_own[...], kern_ext[...]], axis=0)).astype(jnp.bfloat16)

    def ext_back(i, slab):
        return remote(send_ext.at[i], got_ext.at[slab], back_send.at[i], back_recv.at[slab], at(i, outer))

    def own_back(i, slab):
        return remote(send_own.at[i], got_own.at[slab], own_send.at[i], own_recv.at[slab], at(i, b))

    def from_own(i, carry):
        value = jnp.dot(mixed, beside(near_own, two(i)), preferred_element_type=jnp.float32)
        exchanged[i] = value[:rows]
        for n, to in enumerate(two(i)):
            send_ext[to] = value[rows:, n * width : (n + 1) * width].astype(jnp.bfloat16)
            pl.when(inside)(ext_back(to, c).start)
        return carry

    lax.fori_loop(0, nc // 2, from_own, 0)

    for kind in range(nc):
        for r in parts:
            pass_copy(kind, r).wait()
    density_par = lax.dot_general(
        beside(near_own, range(nc), my_rows), beside(near_par, range(nc)), nt, preferred_element_type=jnp.float32
    )
    mixed_par = (density_par * kern_par[...]).astype(jnp.bfloat16)

    def from_par(i, carry):
        value = exchanged[i] + jnp.dot(mixed_par, beside(near_par, two(i)), preferred_element_type=jnp.float32)
        for n, to in enumerate(two(i)):
            send_own[to] = value[:, n * width : (n + 1) * width].astype(jnp.bfloat16)
            pl.when(to != c)(own_back(to, c).start)
        return carry

    lax.fori_loop(0, nc // 2, from_par, 0)
    got_own[c] = send_own[c]

    def finish(i, carry):
        @pl.when(i != c)
        def _():
            own_back(i, i).wait()

        @pl.when(inside)
        def _():
            ext_back(i, i).wait()

        return carry

    lax.fori_loop(0, nc, finish, 0)
    for kind in range(len(leaves)):
        for r in range(ROW_PARTS):
            if kind > 2 or r >= ROW_PARTS - 2:
                field_copy(kind, r).wait_send()

    for i in range(nc):
        total = got_own[i].astype(jnp.float32)
        beyond = got_ext[i].astype(jnp.float32)
        total = total + jnp.where(inside, beyond, jnp.zeros_like(beyond))
        at_i = slice(i * rows, (i + 1) * rows)
        weighted[at_i] = (total * columns[0, at_i, 3:4] * (1.0 / math.sqrt(3 * points))).astype(jnp.bfloat16)

    turned = jnp.concatenate([weighted[i * 128 : (i + 1) * 128, :].T for i in range(points // 128)], axis=1)
    group = 3
    for s in range(LISTED // group):
        value = jnp.dot(
            turned, basis[:, s * group * PANEL_ROWS : (s + 1) * group * PANEL_ROWS], preferred_element_type=jnp.float32
        ) * (1.0 / math.sqrt(points))
        for i in range(group):
            tiles[s * group + i] = value[:, i * PANEL_ROWS : (i + 1) * PANEL_ROWS]

    order = (diagonal, same, ahead, behind, 0)
    DIAGONAL, SAME, AHEAD, BEHIND, HERE = range(5)

    def comb_copy(i):
        return remote(to_mate.at[i], from_mate.at[i], comb_send.at[i], comb_recv.at[i], at(c, mate))

    def part_of(buffer, i, h):
        return buffer.at[i, pl.ds(h, 1)]

    def final_copy(i, h):
        to = (behind if h in near_parts else same) if i == DIAGONAL else order[i]
        return remote(
            part_of(to_owner, i, h), part_of(from_owner, i, h), final_send.at[i, h], final_recv.at[i, h], at(c, pair(to))
        )

    def combine(i, h, merge=False):
        total = tiles[inverse[PANELS_DEV * (4 + 2 * order[i] + k) + h]] + from_mate[i, h].astype(jnp.float32)
        if merge:
            term = from_owner[DIAGONAL, h].astype(jnp.float32)
            total = total + jnp.where(has_ahead, term, jnp.zeros_like(term))
        if i == HERE:
            out_ref[h] = total
        else:
            to_owner[i, h] = total.astype(jnp.bfloat16)

    for i, d in enumerate(order):
        for j in range(PANELS_DEV):
            to_mate[i, j] = tiles[inverse[PANELS_DEV * (5 + 2 * d - k) + j]].astype(jnp.bfloat16)
        comb_copy(i).start()

    comb_copy(DIAGONAL).wait()
    for h in (3, 0, 4, 1, 2):
        combine(DIAGONAL, h)
        pl.when(has_behind)(final_copy(DIAGONAL, h).start)
    comb_copy(SAME).wait()
    for h in far_parts:
        combine(SAME, h)
        final_copy(SAME, h).start()
    comb_copy(AHEAD).wait()
    for h in near_parts:
        combine(AHEAD, h)
        pl.when(has_ahead)(final_copy(AHEAD, h).start)
    comb_copy(BEHIND).wait()
    for h in every:
        combine(BEHIND, h)
        pl.when(has_behind)(final_copy(BEHIND, h).start)
    comb_copy(HERE).wait()
    for h in every:
        combine(HERE, h)
    for h in near_parts:
        pl.when(has_ahead)(final_copy(DIAGONAL, h).wait_recv)
        combine(SAME, h, merge=True)
        final_copy(SAME, h).start()

    @pl.when(has_ahead)
    def _():
        for h in far_parts:
            final_copy(DIAGONAL, h).wait_recv()
            combine(AHEAD, h, merge=True)
            final_copy(AHEAD, h).start()

    for i, sent in ((BEHIND, has_ahead), (SAME, None), (AHEAD, has_behind)):
        for h in every:
            if sent is None:
                final_copy(i, h).wait_recv()
            else:
                pl.when(sent)(final_copy(i, h).wait_recv)
        for j in range(PANELS_DEV):
            term = from_owner[i, j].astype(jnp.float32)
            out_ref[j] += term if sent is None else jnp.where(sent, term, jnp.zeros_like(term))
    results = [pltpu.make_async_copy(out_ref.at[j], out_hbm.at[j], local_sem.at[j]) for j in range(PANELS_DEV)]
    for j, result in enumerate(results):
        out_ref[j] = out_ref[j].T
        result.start()
    for h in every:
        final_copy(SAME, h).wait_send()
        pl.when(has_ahead)(final_copy(AHEAD, h).wait_send)

        @pl.when(has_behind)
        def _(h=h):
            final_copy(DIAGONAL, h).wait_send()
            final_copy(BEHIND, h).wait_send()

    for result in results:
        result.wait()


def solution(mesh):
    nc, ng = mesh.shape["coef"], mesh.shape["grid"]

    def shards(basis_values, occ_coef, listed_panels, centres, point_weights):
        points, functions = basis_values.shape
        width = occ_coef.shape[1]
        rows = points // nc
        bf16, f32 = jnp.bfloat16, jnp.float32
        dma = pltpu.SemaphoreType.DMA
        panel = (PANEL_ROWS, width)
        anywhere = pl.BlockSpec(memory_space=pl.ANY)
        out = pl.pallas_call(
            functools.partial(fused, nc, ng, nc * width),
            out_shape=jax.ShapeDtypeStruct((PANELS_DEV, *panel), f32),
            in_specs=[anywhere] * 5,
            out_specs=anywhere,
            scratch_shapes=[
                pltpu.SMEM((1, LISTED), jnp.int32),
                pltpu.VMEM((PANELS_DEV, *panel), f32),
                pltpu.VMEM((points, functions), bf16),
                pltpu.VMEM((10 * PANELS_DEV, *panel), bf16),
                pltpu.VMEM((functions, width), bf16),
                pltpu.VMEM((3, 8, points), f32),
                pltpu.VMEM((3, points, 8), f32),
                pltpu.SMEM((10 * PANELS_DEV,), jnp.int32),
                pltpu.VMEM((nc, points, width), bf16),
                pltpu.VMEM((nc, points, width), bf16),
                pltpu.VMEM((nc, rows, width), bf16),
                pltpu.VMEM((nc // 2, rows, 2 * width), f32),
                pltpu.VMEM((rows, points), f32),
                pltpu.VMEM((rows, points), f32),
                pltpu.VMEM((rows, points), f32),
                pltpu.VMEM((nc, rows, width), bf16),
                pltpu.VMEM((nc, rows, width), bf16),
                pltpu.VMEM((nc, rows, width), bf16),
                pltpu.VMEM((nc, rows, width), bf16),
                pltpu.VMEM((points, width), bf16),
                pltpu.VMEM((LISTED + 1, *panel), f32),
                pltpu.VMEM((5, PANELS_DEV, *panel), bf16),
                pltpu.VMEM((5, PANELS_DEV, *panel), bf16),
                pltpu.VMEM((4, PANELS_DEV, *panel), bf16),
                pltpu.VMEM((4, PANELS_DEV, *panel), bf16),
                pltpu.VMEM((points,), f32),
                dma((8,)),
                dma((4, PANELS_DEV)), dma((4, PANELS_DEV)), dma((5, PANELS_DEV)), dma((5, PANELS_DEV)),
                dma((nc, ROW_PARTS)), dma((nc, ROW_PARTS)),
                dma((nc, ROW_PARTS)), dma((nc, ROW_PARTS)),
                dma((nc,)), dma((nc,)),
                dma((nc,)), dma((nc,)), dma((nc,)), dma((nc,)),
                dma((5,)), dma((5,)), dma((4, PANELS_DEV)), dma((4, PANELS_DEV)),
            ],
            compiler_params=pltpu.CompilerParams(
                collective_id=0, has_side_effects=True, vmem_limit_bytes=56 * 2**20
            ),
        )(
            basis_values,
            occ_coef.reshape(PANELS_DEV, *panel),
            listed_panels,
            centres,
            point_weights,
        )
        return out.reshape(PANELS_DEV * PANEL_ROWS, width)

    placed = (P("grid", None), P("grid", "coef"), P("grid", None), P(), P("grid"))
    return jax.shard_map(
        shards, mesh=mesh, in_specs=placed, out_specs=P("grid", "coef"), check_vma=False
    )
```

```python
import functools
import math

import jax
import jax.numpy as jnp
from jax import lax
from jax.experimental import pallas as pl
from jax.experimental.pallas import tpu as pltpu
from jax.sharding import PartitionSpec as P

PANEL_ROWS = 128
PANELS_DEV = 5
LISTED = 21
ROW_PARTS = 4
SPLIT = 3
MESH = pl.DeviceIdType.MESH


def fused(
    nc, ng, orbitals,
    basis_hbm, occ_hbm, listed_hbm, centres_hbm, weights_hbm, out_hbm,
    listed, out_ref, basis, cand, chosen, coords, columns, inverse, near_own, near_par,
    ext_rows, exchanged, kern_own, kern_par, kern_ext, send_own, send_ext, got_own, got_ext,
    weighted, tiles, to_mate, from_mate, to_owner, from_owner, line,
    local_sem, occ_send, occ_recv, mate_send, mate_recv,
    field_send, field_recv, pass_send, pass_recv, ext_send, ext_recv,
    own_send, own_recv, back_send, back_recv,
    comb_send, comb_recv, final_send, final_recv,
):
    points, width = near_own.shape[1:]
    rows = points // nc
    part = points // ROW_PARTS
    c = lax.axis_index("coef")
    b = lax.axis_index("grid")
    k = lax.rem(b, 2)
    mate = b + 1 - 2 * k
    outer = b - 1 + 2 * k
    inside = jnp.logical_and(outer >= 0, outer < ng)

    def at(coef, grid):
        return {"coef": coef, "grid": grid}

    def pair(d):
        return b + 2 * d

    def exists(d):
        return jnp.logical_and(pair(d) >= 0, pair(d) < ng)

    side = 1 - 2 * lax.rem(lax.div(b, 2), 2)
    same, ahead, behind, diagonal = side, 2 * side, -2 * side, -side
    has_ahead, has_behind = exists(ahead), exists(behind)
    near_parts, far_parts = range(SPLIT), range(SPLIT, PANELS_DEV)
    every = range(PANELS_DEV)

    def remote(src, dst, send, recv, to):
        return pltpu.make_async_remote_copy(
            src_ref=src, dst_ref=dst, send_sem=send, recv_sem=recv, device_id=to, device_id_type=MESH
        )

    def coef_of(j):
        return lax.rem(c + j, nc)

    barrier = pltpu.get_barrier_semaphore()
    pl.semaphore_signal(barrier, inc=1, device_id=at(c, mate), device_id_type=MESH)
    pl.semaphore_signal(barrier, inc=1, device_id=at(c, pair(same)), device_id_type=MESH)
    expected = jnp.int32(nc + 1)
    for d, there in ((ahead, has_ahead), (behind, has_behind)):
        @pl.when(there)
        def _(d=d):
            pl.semaphore_signal(barrier, inc=1, device_id=at(c, pair(d)), device_id_type=MESH)

        expected += there.astype(jnp.int32)
    for j in range(1, nc):
        pl.semaphore_signal(barrier, inc=1, device_id=at(coef_of(j), b), device_id_type=MESH)

    @pl.when(inside)
    def _():
        for j in range(nc):
            pl.semaphore_signal(barrier, inc=1, device_id=at(coef_of(j), outer), device_id_type=MESH)

    expected += inside.astype(jnp.int32) * nc

    loads = [
        pltpu.make_async_copy(basis_hbm, basis, local_sem.at[0]),
        pltpu.make_async_copy(occ_hbm, cand.at[pl.ds(PANELS_DEV * (4 + k), PANELS_DEV)], local_sem.at[1]),
        pltpu.make_async_copy(centres_hbm.at[:, pl.ds(pl.multiple_of(b * points, 128), points)], coords.at[0, pl.ds(0, 3)], local_sem.at[2]),
        pltpu.make_async_copy(centres_hbm.at[:, pl.ds(pl.multiple_of(mate * points, 128), points)], coords.at[1, pl.ds(0, 3)], local_sem.at[3]),
        pltpu.make_async_copy(weights_hbm, line, local_sem.at[4]),
        pltpu.make_async_copy(listed_hbm, listed, local_sem.at[6]),
    ]
    coords[...] = jnp.zeros_like(coords)
    for load in loads:
        load.start()
    load_outer = pltpu.make_async_copy(
        centres_hbm.at[:, pl.ds(pl.multiple_of(jnp.clip(outer, 0, ng - 1) * points, 128), points)], coords.at[2, pl.ds(0, 3)], local_sem.at[5]
    )
    load_outer.start()

    pl.semaphore_wait(barrier, expected)

    def panel_slot(d, h):
        return cand.at[pl.ds(PANELS_DEV * (4 + 2 * d + k) + h, 1)]

    def panel_copy(role, h):
        mine = occ_hbm.at[pl.ds(h, 1)]
        src, to, dst = (
            (mine, same, -same),
            (mine, behind, ahead),
            (mine, ahead, behind),
            (panel_slot(same, h), ahead, diagonal) if h in near_parts else (panel_slot(ahead, h), same, same),
        )[role]
        return remote(src, panel_slot(dst, h), occ_send.at[role, h], occ_recv.at[role, h], at(c, pair(to)))

    arrives_from = (same, ahead, behind, diagonal)

    def panel_pass(role, h):
        slot = panel_slot(arrives_from[role], h)
        return remote(slot, slot, mate_send.at[role, h], mate_recv.at[role, h], at(c, mate))

    for h in near_parts:
        panel_copy(0, h).start()

    @pl.when(has_behind)
    def _():
        for h in (*far_parts, *near_parts):
            panel_copy(1, h).start()

    @pl.when(has_ahead)
    def _():
        for h in (*far_parts, *near_parts):
            panel_copy(2, h).start()

    for h in far_parts:
        panel_copy(0, h).start()
    whole_slot = cand.at[pl.ds(PANELS_DEV * (4 + k), PANELS_DEV)]
    panel_mate = remote(occ_hbm, whole_slot, mate_send.at[4, 0], mate_recv.at[4, 0], at(c, mate))
    panel_mate.start()

    for load in loads:
        load.wait()
    load_outer.wait()
    coords[0, 3:4] = line[...].reshape(1, points)

    for i in (0, 2):
        columns[i] = coords[i].T

    def distances(left, right, out):
        mine = columns[left, pl.ds(pl.multiple_of(c * rows, 8), rows), :]
        total = None
        for axis in range(3):
            gap = mine[:, axis : axis + 1] - coords[right, axis : axis + 1, :]
            total = gap * gap if total is None else total + gap * gap
        out[...] = lax.rsqrt(total + 0.25) * (1.0 / math.sqrt(orbitals))

    distances(0, 0, kern_own)
    distances(0, 1, kern_par)
    distances(2, 0, kern_ext)

    first = (b - k - 4) * PANELS_DEV

    def panel_here(role, h):
        panel_copy(role, h).wait_recv()
        panel_pass(role, h).start()

    for h in near_parts:
        panel_here(0, h)
        pl.when(has_ahead)(panel_copy(3, h).start)

    @pl.when(has_ahead)
    def _():
        for h in far_parts:
            panel_here(1, h)
            panel_copy(3, h).start()

    @pl.when(has_behind)
    def _():
        for h in far_parts:
            panel_here(2, h)

    for h in far_parts:
        panel_here(0, h)

    @pl.when(has_ahead)
    def _():
        for h in near_parts:
            panel_here(1, h)

    @pl.when(has_behind)
    def _():
        for h in near_parts:
            panel_here(2, h)
        for h in every:
            panel_here(3, h)

    panel_mate.wait()
    for h in every:
        panel_pass(0, h).wait()
        panel_copy(0, h).wait_send()

    @pl.when(has_ahead)
    def _():
        for h in every:
            panel_pass(1, h).wait()
            panel_copy(2, h).wait_send()
            panel_copy(3, h).wait_send()

    @pl.when(has_behind)
    def _():
        for h in every:
            panel_pass(2, h).wait()
            panel_pass(3, h).wait()
            panel_copy(1, h).wait_send()

    def choose(s, carry):
        chosen[pl.ds(pl.multiple_of(s * PANEL_ROWS, 128), PANEL_ROWS), :] = cand[jnp.clip(listed[0, s] - first, 0, 10 * PANELS_DEV - 1)]
        return carry

    lax.fori_loop(0, LISTED, choose, 0)

    across = c + 1 - 2 * lax.rem(c, 2)
    up = lax.rem(c + 2, nc)
    down = lax.rem(c + nc - 2, nc)
    far = lax.rem(c + 4, nc)

    def other(slab):
        return slab + 1 - 2 * lax.rem(slab, 2)

    arrives = (down, up, across, far, other(down), other(up), other(far), c)
    leaves = (
        (c, up), (c, down), (c, across), None, (across, up), (across, down), (far, across),
    )

    def piece(buffer, slab, r):
        return buffer.at[slab, pl.ds(r * part, part)]

    def field_copy(kind, r):
        slab, to = leaves[kind] or ((down, up) if r % 2 == 0 else (up, down))
        return remote(
            piece(near_own, slab, r), piece(near_own, slab, r),
            field_send.at[kind, r], field_recv.at[kind, r], at(to, b),
        )

    def pass_copy(kind, r):
        slab = arrives[kind]
        return remote(
            piece(near_own, slab, r), piece(near_par, slab, r),
            pass_send.at[kind, r], pass_recv.at[kind, r], at(c, mate),
        )

    my_rows = pl.ds(pl.multiple_of(c * rows, 16), rows)

    holders = (up, down, across, far, other(up), other(down), other(far), c)

    def ext_copy(kind):
        to = holders[kind]
        to_rows = pl.ds(pl.multiple_of(to * rows, 16), rows)
        return remote(near_own.at[c, to_rows], ext_rows.at[c], ext_send.at[kind], ext_recv.at[kind], at(to, outer))

    def arrived(kind, r, forward=()):
        field_copy(kind, r).wait_recv()
        for onward in forward:
            field_copy(onward, r).start()
        pass_copy(kind, r).start()

    for r in range(ROW_PARTS):
        near_own[c, r * part : (r + 1) * part] = jnp.dot(
            basis[r * part : (r + 1) * part], chosen[...], preferred_element_type=jnp.float32
        ).astype(jnp.bfloat16)
        for kind in (0, 1, 2):
            if r >= 2:
                field_copy(kind, r - 2).wait_send()
            field_copy(kind, r).start()
        pass_copy(7, r).start()
    for kind in range(nc):
        pl.when(inside)(ext_copy(kind).start)

    def invert(q, carry):
        slot = jnp.int32(LISTED)
        for s in range(LISTED):
            slot = jnp.where(listed[0, s] - first == q, s, slot)
        inverse[q] = slot
        return carry

    lax.fori_loop(0, 10 * PANELS_DEV, invert, 0)
    tiles[LISTED] = jnp.zeros_like(tiles[LISTED])

    parts = range(ROW_PARTS)
    for r in parts:
        arrived(0, r, (3,) if r % 2 == 0 else ())
        arrived(1, r, (3,) if r % 2 == 1 else ())
    for r in parts:
        arrived(2, r, (4, 5))
    for r in parts:
        arrived(3, r, (6,))
    for r in parts:
        arrived(4, r)
        arrived(5, r)
    for r in parts:
        arrived(6, r)

    nt = (((1,), (1,)), ((), ()))

    def beside(ref, slabs, at_rows=slice(None)):
        return jnp.concatenate([ref[slab, at_rows, :] for slab in slabs], axis=1)

    def two(n):
        place = lax.rem(lax.div(c, 2) + jnp.where(n < 2, n + 2, 3 - n), nc // 2)
        return (2 * place, 2 * place + 1)

    @pl.when(inside)
    def _():
        for kind in range(nc):
            ext_copy(kind).wait()

    mine = beside(near_own, range(nc), my_rows)
    both = jnp.concatenate([mine, beside(ext_rows, range(nc))], axis=0)
    density = lax.dot_general(both, beside(near_own, range(nc)), nt, preferred_element_type=jnp.float32)
    mixed = (density * jnp.concatenate([kern_own[...], kern_ext[...]], axis=0)).astype(jnp.bfloat16)

    def ext_back(i, slab):
        return remote(send_ext.at[i], got_ext.at[slab], back_send.at[i], back_recv.at[slab], at(i, outer))

    def own_back(i, slab):
        return remote(send_own.at[i], got_own.at[slab], own_send.at[i], own_recv.at[slab], at(i, b))

    def from_own(i, carry):
        value = jnp.dot(mixed, beside(near_own, two(i)), preferred_element_type=jnp.float32)
        exchanged[i] = value[:rows]
        for n, to in enumerate(two(i)):
            send_ext[to] = value[rows:, n * width : (n + 1) * width].astype(jnp.bfloat16)
            pl.when(inside)(ext_back(to, c).start)
        return carry

    lax.fori_loop(0, nc // 2, from_own, 0)

    for kind in range(nc):
        for r in parts:
            pass_copy(kind, r).wait()
    density_par = lax.dot_general(
        beside(near_own, range(nc), my_rows), beside(near_par, range(nc)), nt, preferred_element_type=jnp.float32
    )
    mixed_par = (density_par * kern_par[...]).astype(jnp.bfloat16)

    def from_par(i, carry):
        value = exchanged[i] + jnp.dot(mixed_par, beside(near_par, two(i)), preferred_element_type=jnp.float32)
        for n, to in enumerate(two(i)):
            send_own[to] = value[:, n * width : (n + 1) * width].astype(jnp.bfloat16)
            pl.when(to != c)(own_back(to, c).start)
        return carry

    lax.fori_loop(0, nc // 2, from_par, 0)
    got_own[c] = send_own[c]

    def finish(i, carry):
        @pl.when(i != c)
        def _():
            own_back(i, i).wait()

        @pl.when(inside)
        def _():
            ext_back(i, i).wait()

        return carry

    lax.fori_loop(0, nc, finish, 0)
    for kind in range(len(leaves)):
        for r in range(ROW_PARTS):
            if kind > 2 or r >= ROW_PARTS - 2:
                field_copy(kind, r).wait_send()

    for i in range(nc):
        total = got_own[i].astype(jnp.float32)
        beyond = got_ext[i].astype(jnp.float32)
        total = total + jnp.where(inside, beyond, jnp.zeros_like(beyond))
        at_i = slice(i * rows, (i + 1) * rows)
        weighted[at_i] = (total * columns[0, at_i, 3:4] * (1.0 / math.sqrt(3 * points))).astype(jnp.bfloat16)

    turned = jnp.concatenate([weighted[i * 128 : (i + 1) * 128, :].T for i in range(points // 128)], axis=1)
    group = 3
    for s in range(LISTED // group):
        value = jnp.dot(
            turned, basis[:, s * group * PANEL_ROWS : (s + 1) * group * PANEL_ROWS], preferred_element_type=jnp.float32
        ) * (1.0 / math.sqrt(points))
        for i in range(group):
            tiles[s * group + i] = value[:, i * PANEL_ROWS : (i + 1) * PANEL_ROWS]

    order = (diagonal, same, ahead, behind, 0)
    DIAGONAL, SAME, AHEAD, BEHIND, HERE = range(5)

    def comb_copy(i):
        return remote(to_mate.at[i], from_mate.at[i], comb_send.at[i], comb_recv.at[i], at(c, mate))

    def part_of(buffer, i, h):
        return buffer.at[i, pl.ds(h, 1)]

    def final_copy(i, h):
        to = (behind if h in near_parts else same) if i == DIAGONAL else order[i]
        return remote(
            part_of(to_owner, i, h), part_of(from_owner, i, h), final_send.at[i, h], final_recv.at[i, h], at(c, pair(to))
        )

    def combine(i, h, merge=False):
        total = tiles[inverse[PANELS_DEV * (4 + 2 * order[i] + k) + h]] + from_mate[i, h].astype(jnp.float32)
        if merge:
            term = from_owner[DIAGONAL, h].astype(jnp.float32)
            total = total + jnp.where(has_ahead, term, jnp.zeros_like(term))
        if i == HERE:
            out_ref[h] = total
        else:
            to_owner[i, h] = total.astype(jnp.bfloat16)

    for i, d in enumerate(order):
        for j in range(PANELS_DEV):
            to_mate[i, j] = tiles[inverse[PANELS_DEV * (5 + 2 * d - k) + j]].astype(jnp.bfloat16)
        comb_copy(i).start()

    comb_copy(DIAGONAL).wait()
    for h in (3, 0, 4, 1, 2):
        combine(DIAGONAL, h)
        pl.when(has_behind)(final_copy(DIAGONAL, h).start)
    comb_copy(SAME).wait()
    for h in far_parts:
        combine(SAME, h)
        final_copy(SAME, h).start()
    comb_copy(AHEAD).wait()
    for h in near_parts:
        combine(AHEAD, h)
        pl.when(has_ahead)(final_copy(AHEAD, h).start)
    comb_copy(BEHIND).wait()
    for h in every:
        combine(BEHIND, h)
        pl.when(has_behind)(final_copy(BEHIND, h).start)
    comb_copy(HERE).wait()
    for h in every:
        combine(HERE, h)
    for h in near_parts:
        pl.when(has_ahead)(final_copy(DIAGONAL, h).wait_recv)
        combine(SAME, h, merge=True)
        final_copy(SAME, h).start()

    @pl.when(has_ahead)
    def _():
        for h in far_parts:
            final_copy(DIAGONAL, h).wait_recv()
            combine(AHEAD, h, merge=True)
            final_copy(AHEAD, h).start()

    for i, sent in ((BEHIND, has_ahead), (SAME, None), (AHEAD, has_behind)):
        for h in every:
            if sent is None:
                final_copy(i, h).wait_recv()
            else:
                pl.when(sent)(final_copy(i, h).wait_recv)
        for j in range(PANELS_DEV):
            term = from_owner[i, j].astype(jnp.float32)
            out_ref[j] += term if sent is None else jnp.where(sent, term, jnp.zeros_like(term))
    results = [pltpu.make_async_copy(out_ref.at[j], out_hbm.at[j], local_sem.at[j]) for j in range(PANELS_DEV)]
    for j, result in enumerate(results):
        out_ref[j] = out_ref[j].T
        result.start()
    for h in every:
        final_copy(SAME, h).wait_send()
        pl.when(has_ahead)(final_copy(AHEAD, h).wait_send)

        @pl.when(has_behind)
        def _(h=h):
            final_copy(DIAGONAL, h).wait_send()
            final_copy(BEHIND, h).wait_send()

    for result in results:
        result.wait()


def solution(mesh):
    nc, ng = mesh.shape["coef"], mesh.shape["grid"]

    def shards(basis_values, occ_coef, listed_panels, centres, point_weights):
        points, functions = basis_values.shape
        width = occ_coef.shape[1]
        rows = points // nc
        bf16, f32 = jnp.bfloat16, jnp.float32
        dma = pltpu.SemaphoreType.DMA
        panel = (PANEL_ROWS, width)
        anywhere = pl.BlockSpec(memory_space=pl.ANY)
        out = pl.pallas_call(
            functools.partial(fused, nc, ng, nc * width),
            out_shape=jax.ShapeDtypeStruct((PANELS_DEV, *panel), f32),
            in_specs=[anywhere] * 5,
            out_specs=anywhere,
            scratch_shapes=[
                pltpu.SMEM((1, LISTED), jnp.int32),
                pltpu.VMEM((PANELS_DEV, *panel), f32),
                pltpu.VMEM((points, functions), bf16),
                pltpu.VMEM((10 * PANELS_DEV, *panel), bf16),
                pltpu.VMEM((functions, width), bf16),
                pltpu.VMEM((3, 8, points), f32),
                pltpu.VMEM((3, points, 8), f32),
                pltpu.SMEM((10 * PANELS_DEV,), jnp.int32),
                pltpu.VMEM((nc, points, width), bf16),
                pltpu.VMEM((nc, points, width), bf16),
                pltpu.VMEM((nc, rows, width), bf16),
                pltpu.VMEM((nc // 2, rows, 2 * width), f32),
                pltpu.VMEM((rows, points), f32),
                pltpu.VMEM((rows, points), f32),
                pltpu.VMEM((rows, points), f32),
                pltpu.VMEM((nc, rows, width), bf16),
                pltpu.VMEM((nc, rows, width), bf16),
                pltpu.VMEM((nc, rows, width), bf16),
                pltpu.VMEM((nc, rows, width), bf16),
                pltpu.VMEM((points, width), bf16),
                pltpu.VMEM((LISTED + 1, *panel), f32),
                pltpu.VMEM((5, PANELS_DEV, *panel), bf16),
                pltpu.VMEM((5, PANELS_DEV, *panel), bf16),
                pltpu.VMEM((4, PANELS_DEV, *panel), bf16),
                pltpu.VMEM((4, PANELS_DEV, *panel), bf16),
                pltpu.VMEM((points,), f32),
                dma((8,)),
                dma((4, PANELS_DEV)), dma((4, PANELS_DEV)), dma((5, PANELS_DEV)), dma((5, PANELS_DEV)),
                dma((nc, ROW_PARTS)), dma((nc, ROW_PARTS)),
                dma((nc, ROW_PARTS)), dma((nc, ROW_PARTS)),
                dma((nc,)), dma((nc,)),
                dma((nc,)), dma((nc,)), dma((nc,)), dma((nc,)),
                dma((5,)), dma((5,)), dma((4, PANELS_DEV)), dma((4, PANELS_DEV)),
            ],
            compiler_params=pltpu.CompilerParams(
                collective_id=0, has_side_effects=True, vmem_limit_bytes=56 * 2**20
            ),
        )(
            basis_values,
            occ_coef.reshape(PANELS_DEV, *panel),
            listed_panels,
            centres,
            point_weights,
        )
        return out.reshape(PANELS_DEV * PANEL_ROWS, width)

    placed = (P("grid", None), P("grid", "coef"), P("grid", None), P(), P("grid"))
    return jax.shard_map(
        shards, mesh=mesh, in_specs=placed, out_specs=P("grid", "coef"), check_vma=False
    )
```
